32 devices in a mesh: rep: 8 (over z, x), shard: 4 (over y, core).
Axes of the slice: x: 2, y: 2, z: 4, core: 2. Of those that a mesh axis runs over, the one named last changes fastest.
Arguments:
- tokens: bfloat16 [32, 577, 1024], P(('rep', 'shard')), may hold values from -6 to 6
- out_grad: bfloat16 [32, 577, 1024], P(('rep', 'shard')), may hold values from -6 to 6
- valid: int32 [32], P(('rep', 'shard')), may hold values 0 or 1
- attn_norm_gain: bfloat16 [1024], P('shard'), may hold values from 0.5 to 1.5
- attn_norm_bias: bfloat16 [1024], P('shard'), may hold values from -3 to 3
- qkv_weight: bfloat16 [1024, 3072], P('shard'), may hold values from -0.1875 to 0.1875
- qv_bias: bfloat16 [2048], P('shard'), may hold values from -3 to 3
- out_weight: bfloat16 [1024, 1024], P('shard'), may hold values from -4 to 4
- out_bias: bfloat16 [1024], P('shard'), may hold values from -3 to 3
- mlp_norm_gain: bfloat16 [1024], P('shard'), may hold values from 0.5 to 1.5
- mlp_norm_bias: bfloat16 [1024], P('shard'), may hold values from -3 to 3
- up_weight: bfloat16 [1024, 4096], P('shard'), may hold values from -0.1875 to 0.1875
- up_bias: bfloat16 [4096], P('shard'), may hold values from -3 to 3
- down_weight: bfloat16 [4096, 1024], P('shard'), may hold values from -0.09375 to 0.09375
- down_bias: bfloat16 [1024], P('shard'), may hold values from -3 to 3
Outputs:
- mixed: bfloat16 [32, 577, 1024], P(('rep', 'shard'))
- token_grad: bfloat16 [32, 577, 1024], P(('rep', 'shard'))
- grad_attn_norm_gain: float32 [1024], P('shard')
- grad_attn_norm_bias: float32 [1024], P('shard')
- grad_qkv_weight: float32 [1024, 3072], P('shard')
- grad_qv_bias: float32 [2048], P('shard')
- grad_out_weight: float32 [1024, 1024], P('shard')
- grad_out_bias: float32 [1024], P('shard')
- grad_mlp_norm_gain: float32 [1024], P('shard')
- grad_mlp_norm_bias: float32 [1024], P('shard')
- grad_up_weight: float32 [1024, 4096], P('shard')
- grad_up_bias: float32 [4096], P('shard')
- grad_down_weight: float32 [4096, 1024], P('shard')
- grad_down_bias: float32 [1024], P('shard')
The draws below stay inside these ranges and needn't reach their ends.
All inputs are finite; a program needn't handle non-finite values. No bound on the sum of `valid` on one device may be relied on, other than what follows from the above.
Results may differ from the reference program's by a relative error of at most 0.012.
Values may be sent and summed in bfloat16 or wider, within the bound.
No kernel may reach another device: no remote copies, remote signals or barrier semaphores. Data moves between devices by JAX's collectives and lax.ppermute only.
A program may use at most 192 MiB of HBM per device.

```python
import jax
import jax.numpy as jnp
from jax import lax

D = 1024
FF = 4096
HEADS = 16
HEAD_DIM = 64
SEQ = 577
IMAGES = 32


def with_ends(array, stream_key, low, largest):
    longest = array.shape.index(max(array.shape))
    spots = []
    for shift in (0, 1):
        where = [jax.random.randint(jax.random.fold_in(stream_key, axis), (), 0, length) for axis, length in enumerate(array.shape)]
        where[longest] = (where[longest] + shift) % array.shape[longest]
        spots.append(tuple(where))
    return array.at[spots[0]].set(low).at[spots[1]].set(largest)


def level_of(rng, shape, pieces, smallest, largest):
    gain, own = 1.0, jax.random.fold_in(rng, 6)
    for position, parts in pieces:
        heights = jnp.exp(jax.random.uniform(jax.random.fold_in(own, position), (parts,), jnp.float32, smallest / len(pieces), largest / len(pieces)))
        gain = gain * jnp.repeat(heights, shape[position] // parts).reshape([-1 if axis == position else 1 for axis in range(len(shape))])
    return gain


def gaussian(rng, dims, width, reach, cuts=(), dtype=jnp.bfloat16):
    result = width * jax.random.normal(rng, dims, jnp.float32)
    if cuts:
        result = result * level_of(rng, dims, cuts, -0.22, 0.18)
    return jnp.clip(result, -reach, reach).astype(dtype)


def setup_inputs(seed: int = 0) -> dict:
    keys = jax.random.split(jax.random.key(seed), 16)
    return {
        "tokens": gaussian(keys[0], (IMAGES, SEQ, D), 1.0, 6.0, ((0, 32),)),
        "out_grad": gaussian(keys[1], (IMAGES, SEQ, D), 1.0, 6.0, ((0, 32),)),
        "valid": with_ends((jax.random.randint(keys[2], (IMAGES,), 0, 4) < 3).astype(jnp.int32), jax.random.fold_in(keys[2], 1), 0, 1),
        "attn_norm_gain": jnp.clip(1.0 + 0.1 * jax.random.normal(keys[3], (D,), jnp.float32), 0.5, 1.5).astype(jnp.bfloat16),
        "attn_norm_bias": gaussian(keys[4], (D,), 0.3, 3.0, ((0, 4),)),
        "qkv_weight": gaussian(keys[5], (D, 3 * D), D ** -0.5, 0.1875, ((0, 4),)),
        "qv_bias": gaussian(keys[6], (2 * D,), 0.5, 3.0, ((0, 4),)),
        "out_weight": gaussian(keys[7], (D, D), 2 ** -0.5, 4.0, ((0, 4),)),
        "out_bias": gaussian(keys[8], (D,), 0.5, 3.0, ((0, 4),)),
        "mlp_norm_gain": jnp.clip(1.0 + 0.1 * jax.random.normal(keys[9], (D,), jnp.float32), 0.5, 1.5).astype(jnp.bfloat16),
        "mlp_norm_bias": gaussian(keys[10], (D,), 0.3, 3.0, ((0, 4),)),
        "up_weight": gaussian(keys[11], (D, FF), D ** -0.5, 0.1875, ((0, 4),)),
        "up_bias": gaussian(keys[12], (FF,), 0.5, 3.0, ((0, 4),)),
        "down_weight": gaussian(keys[13], (FF, D), FF ** -0.5, 0.09375, ((0, 4),)),
        "down_bias": gaussian(keys[14], (D,), 0.5, 3.0, ((0, 4),)),
    }


EPSILON = 1e-06

@jax.custom_vjp
def low(v):
    return lax.optimization_barrier(v.astype(jnp.bfloat16)).astype(jnp.float32)

@jax.custom_vjp
def low_back(v):
    return v

def low_keep(v):
    return (low(v), None)

def low_pass(kept, grad):
    return (grad,)

def back_keep(v):
    return (v, None)

def back_low(kept, grad):
    return (low(grad),)
low.defvjp(low_keep, low_pass)
low_back.defvjp(back_keep, back_low)

def matmul(left, right):
    return jnp.dot(left, right, precision=lax.Precision.HIGHEST)

def layer_norm(values, gain_vec, bias_vec):
    average = lax.optimization_barrier(jnp.mean(values, -1, keepdims=True))
    centered = values - average
    variance = lax.optimization_barrier(jnp.mean(centered * centered, -1, keepdims=True))
    return centered * lax.rsqrt(variance + EPSILON) * gain_vec + bias_vec

def layer_image(one_image, weights_all):
    attn_gain, attn_bias, qkv_w, qv_b, out_w, out_b, mlp_gain, mlp_bias, up_w, up_b, down_w, down_b = weights_all
    model_width = one_image.shape[1]
    normed_one = low(layer_norm(one_image, attn_gain, attn_bias))
    full_bias = jnp.concatenate([qv_b[:model_width], jnp.zeros((model_width,), jnp.float32), qv_b[model_width:]])
    raw_proj = low(low_back(matmul(normed_one, qkv_w) + full_bias))
    split_proj = raw_proj.reshape(SEQ, 3, HEADS, HEAD_DIM)
    query_part = split_proj[:, 0]
    key_part = split_proj[:, 1]
    value_part = split_proj[:, 2]
    scores = jnp.einsum('qhd,khd->hqk', query_part, key_part, precision=lax.Precision.HIGHEST) / jnp.sqrt(jnp.float32(HEAD_DIM))
    scores = low_back(scores)
    probs = low(jax.nn.softmax(scores, axis=-1))
    attended = jnp.einsum('hqk,khd->qhd', probs, value_part, precision=lax.Precision.HIGHEST).reshape(SEQ, model_width)
    attended = low(low_back(attended))
    branch = low_back(matmul(attended, out_w) + out_b)
    middle = one_image + branch
    normed_two = low(layer_norm(middle, mlp_gain, mlp_bias))
    pre_act = low_back(matmul(normed_two, up_w) + up_b)
    activated = low(jax.nn.gelu(pre_act, approximate=False))
    mlp_out = low_back(matmul(activated, down_w) + down_b)
    return middle + mlp_out

def reference(tokens, out_grad, valid, attn_norm_gain, attn_norm_bias, qkv_weight, qv_bias, out_weight, out_bias, mlp_norm_gain, mlp_norm_bias, up_weight, up_bias, down_weight, down_bias):
    weights_all = (attn_norm_gain.astype(jnp.float32), attn_norm_bias.astype(jnp.float32), qkv_weight.astype(jnp.float32), qv_bias.astype(jnp.float32), out_weight.astype(jnp.float32), out_bias.astype(jnp.float32), mlp_norm_gain.astype(jnp.float32), mlp_norm_bias.astype(jnp.float32), up_weight.astype(jnp.float32), up_bias.astype(jnp.float32), down_weight.astype(jnp.float32), down_bias.astype(jnp.float32))
    inputs = tokens.astype(jnp.float32)

    def forward(images_in, weights_in):
        stepper = jax.checkpoint(layer_image)
        return lax.map(lambda one_image: stepper(one_image, weights_in), images_in)
    outputs, pullback = jax.vjp(forward, inputs, weights_all)
    cotangent = out_grad.astype(jnp.float32) * valid.astype(jnp.float32)[:, None, None]
    input_grad, weight_grads = pullback(cotangent)
    return (outputs.astype(jnp.bfloat16), input_grad.astype(jnp.bfloat16), weight_grads[0], weight_grads[1], weight_grads[2], weight_grads[3], weight_grads[4], weight_grads[5], weight_grads[6], weight_grads[7], weight_grads[8], weight_grads[9], weight_grads[10], weight_grads[11])
```

```python
import functools
import math

import jax
import jax.numpy as jnp
from jax import lax
from jax.experimental import pallas as pl
from jax.experimental.pallas import tpu as pltpu
from jax.sharding import PartitionSpec as P

HEAD_DIM = 64
PAIR = 2 * HEAD_DIM
EPSILON = 1e-06
BF = jnp.bfloat16
F32 = jnp.float32
NT = ((1,), (1,))
TN = ((0,), (0,))
VMEM_BYTES = 48 << 20


def up32(values):
    return values.astype(F32)


def flip(axis, size, bit):
    pairs = [(i, i ^ bit) for i in range(size)]
    return lambda values: lax.ppermute(values, axis, pairs)


def pick(first, second, index):
    return jnp.where(index == 0, first, second)


def take(values, index, axis):
    return lax.dynamic_index_in_dim(values, index, axis, keepdims=False)


def dot(left, right, contract=((1,), (0,))):
    return lax.dot_general(left, right, (contract, ((), ())), preferred_element_type=F32)


def tie(*values):
    return lax.optimization_barrier(values)


def normalize(values):
    average = jnp.mean(values, -1, keepdims=True)
    centered = values - average
    inverse = lax.rsqrt(jnp.mean(centered * centered, -1, keepdims=True) + EPSILON)
    return centered * inverse, inverse


def norm_back(upstream, normed, inverse, gain):
    scaled = upstream * gain
    return inverse * (
        scaled
        - jnp.mean(scaled, -1, keepdims=True)
        - normed * jnp.mean(scaled * normed, -1, keepdims=True)
    )


def gelu_parts(values):
    phi = 0.5 * (1.0 + lax.erf(values * (1.0 / math.sqrt(2.0))))
    slope = phi + values * jnp.exp(-0.5 * values * values) * (1.0 / math.sqrt(2.0 * math.pi))
    return values * phi, slope


def attend_kernel(seq, tile, raw_ref, out_ref, log_ref):
    n = raw_ref.shape[0]
    lane = lax.broadcasted_iota(jnp.int32, (n, PAIR), 1)
    row = lax.broadcasted_iota(jnp.int32, (n, PAIR), 0)
    keys, values = raw_ref[:, PAIR:2 * PAIR], raw_ref[:, 2 * PAIR:]
    one, zero = jnp.asarray(1, BF), jnp.asarray(0, BF)
    low = jnp.asarray(-1e30, BF)
    mine = [(lane // HEAD_DIM) == h for h in (0, 1)]
    spare = [lane == (1 - h) * HEAD_DIM for h in (0, 1)]
    k_of = [jnp.where(mine[h], keys, jnp.where(spare[h] & (row >= seq), low, zero)) for h in (0, 1)]
    v_of = [jnp.where(mine[h], values, one) for h in (0, 1)]
    jobs = [(t, min(tile, n - t), h) for t in range(0, n, tile) for h in (0, 1)]

    def score(job):
        t, m, h = job
        q = raw_ref[t:t + m, :PAIR] * jnp.asarray(1.0 / math.sqrt(HEAD_DIM), BF)
        q = jnp.where(mine[h][t:t + m], q, jnp.where(spare[h][t:t + m], one, zero))
        return dot(q, k_of[h], NT)

    ahead = 2
    ready = [score(job) for job in jobs[:ahead]]
    for i, (t, m, h) in enumerate(jobs):
        if i + ahead < len(jobs):
            ready.append(score(jobs[i + ahead]))
        s = ready.pop(0)
        top = jnp.max(s, -1, keepdims=True)
        res = dot(jnp.exp(s - top).astype(BF), v_of[h])
        own = slice(h * HEAD_DIM, (h + 1) * HEAD_DIM)
        other = slice((1 - h) * HEAD_DIM, (2 - h) * HEAD_DIM)
        total = res[:, other]
        out_ref[t:t + m, own] = (res[:, own] / total).astype(BF)
        log_ref[t:t + m, own] = top + jnp.log(total)


def attend(raw, seq, images, padded):
    groups = raw.shape[1] // (3 * PAIR)
    spec = pl.BlockSpec((padded, PAIR), lambda i, g: (i, g))
    return pl.pallas_call(
        functools.partial(attend_kernel, seq, 304),
        grid=(images, groups),
        in_specs=[pl.BlockSpec((padded, 3 * PAIR), lambda i, g: (i, g))],
        out_specs=[spec, spec],
        out_shape=[
            jax.ShapeDtypeStruct((images * padded, groups * PAIR), BF),
            jax.ShapeDtypeStruct((images * padded, groups * PAIR), F32),
        ],
        compiler_params=pltpu.CompilerParams(vmem_limit_bytes=VMEM_BYTES),
        cost_estimate=pl.CostEstimate(
            flops=14 << 30, bytes_accessed=raw.size * 4, transcendentals=0),
        name="attend",
    )(raw)


def attend_back_kernel(seq, wide, raw_ref, d_ref, log_ref, out_ref, kk_ref, vv_ref, p_ref, s_ref):
    n = raw_ref.shape[0]
    scale = 1.0 / math.sqrt(HEAD_DIM)
    lane = lax.broadcasted_iota(jnp.int32, (n, PAIR), 1)
    zero = jnp.asarray(0, BF)
    gap = jnp.zeros((wide - n, PAIR), BF)

    def stacked(v):
        first = lane < HEAD_DIM
        return jnp.concatenate([jnp.where(first, v, zero), gap, jnp.where(first, zero, v), gap], 0)

    kk_ref[:, :PAIR] = stacked(raw_ref[:, PAIR:2 * PAIR])
    vv_ref[...] = stacked(raw_ref[:, 2 * PAIR:])

    @pl.when((pl.program_id(0) == 0) & (pl.program_id(1) == 0))
    def _():
        lanes = lax.broadcasted_iota(jnp.int32, (2 * wide, PAIR), 1)
        row = lax.broadcasted_iota(jnp.int32, (2 * wide, PAIR), 0)
        row = jnp.where(row >= wide, row - wide, row)
        kk_ref[:, PAIR:] = jnp.where((lanes == 0) & (row >= seq), jnp.asarray(-1e30, BF), zero)

    q = raw_ref[:, :PAIR]
    d = d_ref[...]
    mask = jnp.where(lane == 0, jnp.asarray(1, BF), zero)
    s = dot(jnp.concatenate([q * jnp.asarray(scale, BF), mask], 1), kk_ref[...], NT)
    dp = dot(d, vv_ref[...], NT)
    for h in (0, 1):
        cols = slice(h * wide, (h + 1) * wide)
        p = jnp.exp(s[:, cols] - log_ref[:, h * HEAD_DIM:h * HEAD_DIM + 1])
        dph = dp[:, cols]
        p_ref[:, cols] = p.astype(BF)
        s_ref[:, cols] = (p * (dph - jnp.sum(dph * p, -1, keepdims=True))).astype(BF)
    out_ref[:, :PAIR] = (dot(s_ref[...], kk_ref[:, :PAIR]) * scale).astype(BF)
    dk = dot(s_ref[...], q, TN)
    dv = dot(p_ref[...], d, TN)
    first = lane < HEAD_DIM
    out_ref[:, PAIR:2 * PAIR] = (jnp.where(first, dk[:n], dk[wide:wide + n]) * scale).astype(BF)
    out_ref[:, 2 * PAIR:] = jnp.where(first, dv[:n], dv[wide:wide + n]).astype(BF)


def attend_back(raw, d_att, logs, seq, images, padded):
    groups = raw.shape[1] // (3 * PAIR)
    wide = -(-padded // 128) * 128
    one = pl.BlockSpec((padded, PAIR), lambda i, g: (i, g))
    three = pl.BlockSpec((padded, 3 * PAIR), lambda i, g: (i, g))
    return pl.pallas_call(
        functools.partial(attend_back_kernel, seq, wide),
        grid=(images, groups),
        in_specs=[three, one, one],
        out_specs=three,
        out_shape=jax.ShapeDtypeStruct(raw.shape, BF),
        scratch_shapes=[
            pltpu.VMEM((2 * wide, 2 * PAIR), BF),
            pltpu.VMEM((2 * wide, PAIR), BF),
            pltpu.VMEM((padded, 2 * wide), BF),
            pltpu.VMEM((padded, 2 * wide), BF),
        ],
        compiler_params=pltpu.CompilerParams(vmem_limit_bytes=VMEM_BYTES),
        cost_estimate=pl.CostEstimate(
            flops=28 << 30, bytes_accessed=raw.size * 4, transcendentals=0),
        name="attend_back",
    )(raw, d_att, logs)


TILE = 208


def whole(array):
    return pl.BlockSpec(array.shape, lambda *_: (0,) * array.ndim)


def params():
    return pltpu.CompilerParams(vmem_limit_bytes=VMEM_BYTES)


def at_quarter(index, quarter):
    return pl.ds(pl.multiple_of(index * quarter, quarter), quarter)


def spread_kernel(size, starts_ref, w_ref, own_ref, other_ref):
    count = own_ref.shape[1] // size
    for k, out_ref in enumerate((own_ref, other_ref)):
        for i in range(count):
            start = pl.multiple_of(starts_ref[k * count + i], 128)
            out_ref[:, i * size:(i + 1) * size] = w_ref[:, pl.ds(start, size)]


def spread(w, own_starts, other_starts, size):
    one = jax.ShapeDtypeStruct((w.shape[0], len(own_starts) * size), w.dtype)
    return pl.pallas_call(
        functools.partial(spread_kernel, size),
        grid_spec=pltpu.PrefetchScalarGridSpec(
            num_scalar_prefetch=1, grid=(1,), in_specs=[whole(w)], out_specs=[whole(one)] * 2),
        out_shape=[one] * 2,
        compiler_params=params(),
        name="spread",
    )(jnp.stack(own_starts + other_starts).astype(jnp.int32), w)


def row_mask(tile, seq):
    return lax.broadcasted_iota(jnp.int32, (TILE, 1), 0) + tile * TILE < seq


def enter_kernel(seq, s_ref, own_ref, other_ref, grad_ref, grad2_ref, gain_ref, shift_ref,
                 norm_ref, out_ref, hold_ref):
    images = pl.num_programs(0) // 2
    i = pl.program_id(0)
    ok = row_mask(pl.program_id(1), seq)
    quarter = hold_ref.shape[1] // 4
    mine = i < images
    x = up32(jnp.where(mine, own_ref[0], other_ref[0]))
    unit, _ = normalize(x)
    hold_ref[...] = unit * gain_ref[...] + shift_ref[...]
    for j in range(4):
        value = hold_ref[:, at_quarter(s_ref[0] ^ j, quarter)]
        norm_ref[0, :, j * quarter:(j + 1) * quarter] = jnp.where(ok, value, 0.0).astype(BF)
    grad = jnp.where(mine, grad_ref[0], grad2_ref[0])
    out_ref[0] = jnp.where(ok & (s_ref[1 + i] != 0), up32(grad) * up32(s_ref[1 + i]), 0.0).astype(BF)


def enter(scalars, own, other, grad, grad2, gain, shift, padded):
    images, seq, width = own.shape
    tiles = -(-padded // TILE)
    first = pl.BlockSpec((1, TILE, width), lambda i, t, s: (jnp.minimum(i, images - 1), t, 0))
    second = pl.BlockSpec((1, TILE, width), lambda i, t, s: (jnp.maximum(i - images, 0), t, 0))
    both = pl.BlockSpec((1, TILE, width), lambda i, t, s: (i, t, 0))
    one = jax.ShapeDtypeStruct((2 * images, padded, width), BF)
    return pl.pallas_call(
        functools.partial(enter_kernel, seq),
        grid_spec=pltpu.PrefetchScalarGridSpec(
            num_scalar_prefetch=1, grid=(2 * images, tiles),
            in_specs=[first, second, first, second, whole(gain), whole(shift)],
            out_specs=[both, both], scratch_shapes=[pltpu.VMEM((TILE, width), F32)]),
        out_shape=[one, one],
        compiler_params=params(),
        name="enter",
    )(scalars, own, other, grad, grad2, gain, shift)


def middle_kernel(seq, s_ref, x_ref, own_ref, got_ref, add_ref, gain_ref, shift_ref,
                  mid_ref, mine_ref, theirs_ref, hold_ref):
    ok = row_mask(pl.program_id(1), seq)
    quarter = hold_ref.shape[1] // 4
    middle = up32(x_ref[0]) + own_ref[0] + up32(got_ref[0]) + add_ref[...]
    middle = jnp.where(ok, middle, 0.0)
    mid_ref[0] = middle
    unit, _ = normalize(middle)
    hold_ref[...] = jnp.where(ok, unit * gain_ref[...] + shift_ref[...], 0.0)
    for j in range(4):
        cols = slice(j * quarter, (j + 1) * quarter)
        mine_ref[0, :, cols] = hold_ref[:, at_quarter(s_ref[0] ^ j, quarter)].astype(BF)
        theirs_ref[0, :, cols] = hold_ref[:, at_quarter(s_ref[0] ^ 1 ^ j, quarter)].astype(BF)


def middle_call(scalars, x, own, got, add, gain, shift):
    images, seq, width = x.shape
    padded = own.shape[1]
    block = pl.BlockSpec((1, TILE, width), lambda i, t, s: (i, t, 0))
    vec = whole(gain)
    shape = (images, padded, width)
    return pl.pallas_call(
        functools.partial(middle_kernel, seq),
        grid_spec=pltpu.PrefetchScalarGridSpec(
            num_scalar_prefetch=1, grid=(images, -(-padded // TILE)),
            in_specs=[block, block, block, vec, vec, vec], out_specs=[block] * 3,
            scratch_shapes=[pltpu.VMEM((TILE, width), F32)]),
        out_shape=[jax.ShapeDtypeStruct(shape, F32), jax.ShapeDtypeStruct(shape, BF),
                   jax.ShapeDtypeStruct(shape, BF)],
        compiler_params=params(),
        name="middle",
    )(scalars, x, own, got, add, gain, shift)


def ordered_sum(s_ref, own_ref, got_ref, hold_ref):
    quarter = hold_ref.shape[1] // 4
    for j in range(4):
        cols = slice(j * quarter, (j + 1) * quarter)
        k = j ^ 1
        theirs = slice(k * quarter, (k + 1) * quarter)
        hold_ref[:, at_quarter(s_ref[0] ^ j, quarter)] = (
            own_ref[0, :, cols] + up32(got_ref[0, :, theirs]))
    return hold_ref[...]


def column_sum(value):
    return jnp.sum(value, 0, keepdims=True)


def back_middle_kernel(seq, s_ref, own_ref, got_ref, mid_ref, grad_ref, gain_ref,
                       d_ref, low_ref, sum_ref, hold_ref):
    i, t = pl.program_id(0), pl.program_id(1)
    ok = row_mask(t, seq)
    unit, inverse = normalize(mid_ref[0])
    h = jnp.where(ok, ordered_sum(s_ref, own_ref, got_ref, hold_ref), 0.0)
    unit = jnp.where(ok, unit, 0.0)
    dy = jnp.where(ok & (s_ref[1 + i] != 0), up32(grad_ref[0]) * up32(s_ref[1 + i]), 0.0)
    d_middle = jnp.where(ok, dy + norm_back(h, unit, inverse, gain_ref[...]), 0.0)
    low = d_middle.astype(BF)
    d_ref[0] = d_middle
    low_ref[0] = low

    @pl.when((i == 0) & (t == 0))
    def _():
        sum_ref[...] = jnp.zeros_like(sum_ref)

    sum_ref[0:1, :] += column_sum(h * unit)
    sum_ref[1:2, :] += column_sum(h)
    sum_ref[2:3, :] += column_sum(up32(low))
    sum_ref[3:4, :] += column_sum(up32(dy.astype(BF)))


def back_middle(scalars, own, got, mid, grad, gain):
    images, seq, width = grad.shape
    padded = own.shape[1]
    block = pl.BlockSpec((1, TILE, width), lambda i, t, s: (i, t, 0))
    sums = jax.ShapeDtypeStruct((8, width), F32)
    shape = (images, padded, width)
    return pl.pallas_call(
        functools.partial(back_middle_kernel, seq),
        grid_spec=pltpu.PrefetchScalarGridSpec(
            num_scalar_prefetch=1, grid=(images, -(-padded // TILE)),
            in_specs=[block] * 4 + [whole(gain)], out_specs=[block, block, whole(sums)],
            scratch_shapes=[pltpu.VMEM((TILE, width), F32)]),
        out_shape=[jax.ShapeDtypeStruct(shape, F32), jax.ShapeDtypeStruct(shape, BF), sums],
        compiler_params=params(),
        name="back_middle",
    )(scalars, own, got, mid, grad, gain)


def leave_kernel(seq, s_ref, own_ref, got_ref, x_ref, mid_ref, gain_ref,
                 d_ref, sum_ref, hold_ref):
    i, t = pl.program_id(0), pl.program_id(1)
    ok = row_mask(t, seq)
    unit, inverse = normalize(up32(x_ref[0]))
    h = jnp.where(ok, ordered_sum(s_ref, own_ref, got_ref, hold_ref), 0.0)
    d_ref[0] = (mid_ref[0] + norm_back(h, unit, inverse, gain_ref[...])).astype(BF)

    @pl.when((i == 0) & (t == 0))
    def _():
        sum_ref[...] = jnp.zeros_like(sum_ref)

    sum_ref[0:1, :] += column_sum(jnp.where(ok, h * unit, 0.0))
    sum_ref[1:2, :] += column_sum(h)


def leave(scalars, own, got, x, mid, gain):
    images, seq, width = x.shape
    padded = own.shape[1]
    block = pl.BlockSpec((1, TILE, width), lambda i, t, s: (i, t, 0))
    sums = jax.ShapeDtypeStruct((8, width), F32)
    return pl.pallas_call(
        functools.partial(leave_kernel, seq),
        grid_spec=pltpu.PrefetchScalarGridSpec(
            num_scalar_prefetch=1, grid=(images, -(-padded // TILE)),
            in_specs=[block] * 4 + [whole(gain)], out_specs=[block, whole(sums)],
            scratch_shapes=[pltpu.VMEM((TILE, width), F32)]),
        out_shape=[jax.ShapeDtypeStruct(x.shape, BF), sums],
        compiler_params=params(),
        name="leave",
    )(scalars, own, got, x, mid, gain)


def place_kernel(count, rows, moves, where_ref, *refs):
    ins, out_ref = refs[:count], refs[count]
    for number, row, col, size, to in moves:
        value = up32(ins[number][pl.ds(pl.multiple_of(where_ref[row], 16), rows[1]),
                                 col:col + size])
        to_row, to_col = to
        out_ref[to_row:to_row + rows[1],
                pl.ds(pl.multiple_of(where_ref[to_col], 128), size)] = value


def place(where, inputs, rows, shape, moves):
    out = jax.ShapeDtypeStruct(shape, F32)
    return pl.pallas_call(
        functools.partial(place_kernel, len(inputs), rows, moves),
        grid_spec=pltpu.PrefetchScalarGridSpec(
            num_scalar_prefetch=1, grid=(1,), in_specs=[whole(v) for v in inputs],
            out_specs=whole(out)),
        out_shape=out,
        compiler_params=params(),
        name="place",
    )(jnp.stack([jnp.asarray(w, jnp.int32) for w in where]), *inputs)


def build(mesh):
    reps = mesh.shape["rep"]
    shards = mesh.shape["shard"]
    core_swap = flip("shard", shards, 1)
    y_swap = flip("shard", shards, 2)
    bits = [1 << i for i in range(reps.bit_length() - 1)]
    rep_swap = {b: flip("rep", reps, b) for b in bits}
    x_bit, z_bits = bits[0], bits[1:3]
    rest = bits[3:]

    def per_device(
        tokens, out_grad, valid, attn_gain, attn_shift, qkv_w, qv_b, out_w, out_b,
        mlp_gain, mlp_shift, up_w, up_b, down_w, down_b,
    ):
        images, seq, width = tokens.shape
        ff = up_w.shape[1]
        quarter = width // shards
        half = width // 2
        ffq = ff // shards
        padded = -(-seq // 16) * 16
        rows = images * padded
        shard = lax.axis_index("shard")
        rep = lax.axis_index("rep")
        y, c = shard // 2, shard % 2
        x = rep % 2
        z_at = [(rep // b) % 2 for b in z_bits]
        pairs = quarter // PAIR


        def qkv_starts(of):
            return [part * width + (of ^ side) * quarter + g * PAIR
                    for side in (0, 2) for g in range(pairs) for part in range(3)]

        parts = 2
        fp = ffq // parts

        def up_starts(of):
            return [(of ^ side) * ffq + k * fp for k in range(parts) for side in (0, 2)]

        qkv_own, qkv_give = spread(qkv_w, qkv_starts(shard), qkv_starts(shard ^ 1), PAIR)
        halfc = qkv_own.shape[1] // 2

        def by_x(v):
            return pick(v[:, :v.shape[1] // 2], v[:, v.shape[1] // 2:], x)

        def swap_halves(v):
            h = v.shape[1] // 2
            return jnp.concatenate([v[:, h:], v[:, :h]], 1)

        qkv_other = core_swap(qkv_give)
        far_own = y_swap(by_x(qkv_own))
        tokens2, grad2 = core_swap(tokens), core_swap(out_grad)
        small = jnp.concatenate(
            [attn_gain, attn_shift, qv_b, out_b, mlp_gain, mlp_shift, up_b, down_b])
        small = jnp.stack([small, core_swap(small)])
        up_own, up_give = spread(up_w, up_starts(shard), up_starts(shard ^ 1), fp)
        far_other = y_swap(by_x(qkv_other))
        far_small = y_swap(small)
        up_other = core_swap(up_give)
        far_out = y_swap(out_w)

        far_up, far_down = [], []
        for k in range(parts):
            cols = slice(2 * k * fp, 2 * (k + 1) * fp)
            far_up.append(y_swap(pick(up_own[:, cols], up_other[:, cols], x)))
            piece = down_w[k * fp:(k + 1) * fp]
            far_down.append(y_swap(pick(piece[:fp // 2], piece[fp // 2:], x)))

        small = jnp.concatenate([small, far_small], 0)
        small = jnp.stack([
            pick(pick(small[j], small[j ^ 1], c), pick(small[j ^ 2], small[j ^ 3], c), y)
            for j in range(shards)])
        sizes = [quarter, quarter, 2 * quarter, quarter, quarter, quarter, ffq, quarter]
        cuts = []
        at = 0
        for size in sizes:
            cuts.append(up32(small[:, at:at + size].reshape(1, -1)))
            at += size
        g1, b1, qvb, ob, g2, b2, ub, db = cuts

        scalars = jnp.concatenate(
            [shard[None], valid, core_swap(valid)]).astype(jnp.int32)
        normed1, d_out = enter(scalars, tokens, tokens2, out_grad, grad2, g1, b1, padded)
        normed1 = normed1.reshape(2 * rows, width)
        d_out = d_out.reshape(2 * rows, width)
        bias = jnp.concatenate([qvb[:, :width], jnp.zeros((1, width), F32), qvb[:, width:]], 1)
        bias = jnp.concatenate(
            [lax.dynamic_slice_in_dim(bias, start, PAIR, 1) for start in qkv_starts(shard)], 1)
        upb = [jnp.concatenate(
            [lax.dynamic_slice_in_dim(ub, start, fp, 1) for start in up_starts(shard)[2 * k:2 * k + 2]], 1)
            for k in range(parts)]

        def from_x(got):
            return got, rep_swap[x_bit](got)

        def set_cols(got, swapped):
            return jnp.concatenate([pick(got, swapped, x), pick(swapped, got, x)], 1)

        far_own, far_own2 = from_x(far_own)
        far_other, far_other2 = from_x(far_other)
        far = jnp.concatenate([
            swap_halves(set_cols(far_own, far_own2)), swap_halves(set_cols(far_other, far_other2))], 0)
        qkv_full = jnp.concatenate([qkv_own, qkv_other, far], 0)
        raw = (dot(normed1, qkv_full) + bias).astype(BF)
        attended, logs = attend(raw, seq, 2 * images, padded)

        spine = attended

        def far_up_pair(k):
            return from_x(far_up[k])

        far_up[0], attended = tie(far_up[0], attended)
        ups2 = [from_x(far_up[0])]
        out_full = jnp.concatenate([out_w, far_out], 0)
        part = dot(attended[rows:], out_full).astype(BF)
        got = core_swap(part)
        part = dot(attended[:rows], out_full)

        def cube(v):
            return v.reshape(images, padded, width)

        middle, normed2, give = middle_call(
            scalars, tokens, cube(part), cube(got), ob, g2, b2)
        give = core_swap(give)
        far_down[0], give = tie(far_down[0], give)
        downs2 = [from_x(far_down[0])]
        normed2 = jnp.concatenate([normed2.reshape(rows, width), give.reshape(rows, width)], 0)

        def begin(send):
            return y_swap(send)

        h_parts, acts, downs, up_bias_sums = [], [], [], []
        d_sent, u_sent = [], []
        d_keep, u_keep = [], []
        for k in range(parts):
            cols = slice(2 * k * fp, 2 * (k + 1) * fp)
            a, b = ups2[k]
            up = jnp.concatenate([up_own[:, cols], up_other[:, cols],
                                  swap_halves(pick(a, b, x)), swap_halves(pick(b, a, x))], 0)
            pre = dot(normed2, up) + upb[k]
            act, slope = gelu_parts(pre)
            act = act.astype(BF)
            g_far = dot(act[:, fp:], d_out, TN).astype(BF)
            d_sent.append(begin(g_far))
            d_keep.append(dot(act[:, :fp], d_out, TN).astype(BF))
            a, b = downs2[k]
            down = jnp.concatenate(
                [down_w[k * fp:(k + 1) * fp], pick(a, b, x), pick(b, a, x)], 0)
            d_act = dot(d_out, down, NT)
            d_pre = (d_act * slope).astype(BF)
            up_bias_sums.append(jnp.sum(up32(d_pre), 0))
            g_far = swap_halves(dot(normed2[:, half:], d_pre, TN).astype(BF))
            u_sent.append(begin(g_far))
            u_keep.append(dot(normed2[:, :half], d_pre, TN).astype(BF))
            h_parts.append((d_pre, up))
            acts.append(act)
            downs.append(down)
            if k + 1 < parts:
                far_up[k + 1], d_pre_ = tie(far_up[k + 1], u_keep[k])
                u_keep[k] = d_pre_
                ups2.append(from_x(far_up[k + 1]))
                downs2.append(from_x(far_down[k + 1]))

        h_other = sum(dot(p[rows:], u, NT) for p, u in h_parts).astype(BF)
        h_got = core_swap(h_other)
        h_own = sum(dot(p[:rows], u, NT) for p, u in h_parts)

        def halves(keep, got, bit):
            n = keep.shape[0] // 2
            total = (up32(lax.dynamic_slice_in_dim(keep, (1 - bit) * n, n, 0))
                     + up32(lax.dynamic_slice_in_dim(got, (1 - bit) * n, n, 0))).astype(BF)
            mine = (up32(lax.dynamic_slice_in_dim(keep, bit * n, n, 0))
                    + up32(lax.dynamic_slice_in_dim(got, bit * n, n, 0))).astype(BF)
            return mine, total

        def stage(keep, got, bit, swap, after):
            got, after = tie(got, after)
            mine, theirs = halves(keep, got, bit)
            theirs, after = tie(theirs, after)
            return mine, swap(theirs), after

        def settle(mine, got, after):
            got, after = tie(got, after)
            total = (up32(mine) + up32(got)).astype(BF)
            for b in rest:
                total = (up32(total) + up32(rep_swap[b](total))).astype(BF)
            total, after = tie(total, after)
            return total, after

        def join(a, got, after):
            got, after = tie(got, after)
            a, after = tie(jnp.concatenate([a, got], 0), after)
            return a, after

        d_x, u_x = [None] * parts, [None] * parts
        d_mine, u_mine = [None] * parts, [None] * parts
        d_mine[0], d_x[0], h_own = stage(d_keep[0], d_sent[0], x, rep_swap[x_bit], h_own)

        d_middle, d_branch_own, sums2 = back_middle(
            scalars, cube(h_own), cube(h_got), middle, out_grad, g2)
        d_branch = jnp.concatenate(
            [d_branch_own.reshape(rows, width), core_swap(d_branch_own).reshape(rows, width)], 0)
        d_att = dot(d_branch, out_full, NT).astype(BF)
        out_sent = begin(dot(attended[:, quarter:], d_branch, TN).astype(BF))
        out_keep = dot(attended[:, :quarter], d_branch, TN).astype(BF)
        u_mine[0], u_x[0], d_att = stage(u_keep[0], u_sent[0], x, rep_swap[x_bit], d_att)
        d_raw = attend_back(raw, d_att, logs, seq, 2 * images, padded)

        q_sent, q_keep = [], []
        for k in range(2):
            theirs = slice(halfc, 2 * halfc) if k == 0 else slice(0, halfc)
            mine = slice(0, halfc) if k == 0 else slice(halfc, 2 * halfc)
            q_sent.append(begin(dot(normed1[:, half:], d_raw[:, theirs], TN).astype(BF)))
            q_keep.append(dot(normed1[:, :half], d_raw[:, mine], TN).astype(BF))

        d_mine[1], d_x[1], d_raw = stage(d_keep[1], d_sent[1], x, rep_swap[x_bit], d_raw)

        def merge(k, after):
            gots = tie(d_x[k], u_x[k], after)
            after = gots[2]
            d = (up32(d_mine[k]) + up32(gots[0])).astype(BF)
            u = (up32(u_mine[k]) + up32(gots[1])).astype(BF)
            theirs, after = tie(pick(u, d, z_at[0]), after)
            return pick(d, u, z_at[0]), rep_swap[z_bits[0]](theirs), after

        m_keep, m_got = [None] * parts, [None] * parts
        m_keep[0], m_got[0], d_raw = merge(0, d_raw)
        h_other = dot(d_raw[rows:], qkv_full, NT).astype(BF)
        h_got = core_swap(h_other)
        h_own = dot(d_raw[:rows], qkv_full, NT)
        token_grad, sums1 = leave(scalars, cube(h_own), cube(h_got), tokens, d_middle, g1)
        column_sums = jnp.sum(up32(d_raw), 0)

        def rel(v):
            v = v.reshape(shards, -1)
            return jnp.stack([
                pick(pick(v[j], v[j ^ 1], c), pick(v[j ^ 2], v[j ^ 3], c), y)
                for j in range(shards)])

        def both(v):
            return jnp.stack([v[0], jnp.zeros_like(v[0]), v[1], jnp.zeros_like(v[1])])

        col = column_sums.reshape(2, pairs, 3, PAIR)
        qv = jnp.stack([col[:, :, j].reshape(2, quarter) for j in (0, 2)])
        qv = jnp.stack([qv[:, 0], jnp.zeros_like(qv[:, 0]), qv[:, 1], jnp.zeros_like(qv[:, 0])], 1)
        qv = jnp.concatenate([rel(qv[j]).reshape(-1) for j in (0, 1)])
        up_sum = both(jnp.concatenate([v.reshape(2, fp) for v in up_bias_sums], 1))
        vectors = jnp.concatenate(
            [rel(sums1[0]), rel(sums1[1]), rel(qv), rel(sums2[2]), rel(sums2[0]),
             rel(sums2[1]), up_sum, rel(sums2[3])], 1).reshape(2, 2, -1)
        vec_got = core_swap(vectors[:, 1])
        vectors = vectors[:, 0] + vec_got
        vec_got = y_swap(vectors[1])
        vectors = vectors[0]

        m_other = sum(dot(a[rows:], d) for a, d in zip(acts, downs)).astype(BF)
        m_got_c = core_swap(m_other)
        m_own = sum(dot(a[:rows], d) for a, d in zip(acts, downs))
        mixed = (middle + cube(m_own) + up32(cube(m_got_c)) + db).astype(BF)[:, :seq]

        u_mine[1], u_x[1], mixed = stage(u_keep[1], u_sent[1], x, rep_swap[x_bit], mixed)
        out_mine, out_x, mixed = stage(out_keep, out_sent, x, rep_swap[x_bit], mixed)
        m_keep[0], m_got[0], mixed = stage(m_keep[0], m_got[0], z_at[1], rep_swap[z_bits[1]], mixed)
        m_keep[1], m_got[1], mixed = merge(1, mixed)
        m0, mixed = settle(m_keep[0], m_got[0], mixed)
        got0 = rep_swap[z_bits[1]](m0)
        o_keep, o_got, mixed = stage(out_mine, out_x, z_at[0], rep_swap[z_bits[0]], mixed)
        q_mine, q_x = [None] * 2, [None] * 2
        q_mine[0], q_x[0], mixed = stage(q_keep[0], q_sent[0], x, rep_swap[x_bit], mixed)
        vec_got, mixed = tie(vec_got, mixed)
        vectors, mixed = tie(vectors + vec_got, mixed)
        vec_got = rep_swap[x_bit](vectors)
        m0, mixed = join(m0, got0, mixed)
        got0 = rep_swap[z_bits[0]](m0)
        m_keep[1], m_got[1], mixed = stage(m_keep[1], m_got[1], z_at[1], rep_swap[z_bits[1]], mixed)
        o_keep, o_got, mixed = stage(o_keep, o_got, z_at[1], rep_swap[z_bits[1]], mixed)
        q_mine[1], q_x[1], mixed = stage(q_keep[1], q_sent[1], x, rep_swap[x_bit], mixed)
        q_mine[0], q_x[0], mixed = stage(q_mine[0], q_x[0], z_at[0], rep_swap[z_bits[0]], mixed)
        vec_got, mixed = tie(vec_got, mixed)
        vectors, mixed = tie(vectors + vec_got, mixed)
        vec_got = rep_swap[z_bits[0]](vectors)
        m0, mixed = join(m0, got0, mixed)
        got0 = rep_swap[x_bit](m0)
        m1, mixed = settle(m_keep[1], m_got[1], mixed)
        got1 = rep_swap[z_bits[1]](m1)
        o, mixed = settle(o_keep, o_got, mixed)
        got_o = rep_swap[z_bits[1]](o)
        q_mine[0], q_x[0], mixed = stage(q_mine[0], q_x[0], z_at[1], rep_swap[z_bits[1]], mixed)
        q_mine[1], q_x[1], mixed = stage(q_mine[1], q_x[1], z_at[0], rep_swap[z_bits[0]], mixed)
        m1, mixed = join(m1, got1, mixed)
        got1 = rep_swap[z_bits[0]](m1)
        o, mixed = join(o, got_o, mixed)
        got_o = rep_swap[z_bits[0]](o)
        vec_got, mixed = tie(vec_got, mixed)
        vectors, mixed = tie(vectors + vec_got, mixed)
        vec_got = rep_swap[z_bits[1]](vectors)
        qa, mixed = settle(q_mine[0], q_x[0], mixed)
        got_a = rep_swap[z_bits[1]](qa)
        q_mine[1], q_x[1], mixed = stage(q_mine[1], q_x[1], z_at[1], rep_swap[z_bits[1]], mixed)
        m1, mixed = join(m1, got1, mixed)
        o, mixed = join(o, got_o, mixed)
        got1 = rep_swap[x_bit](m1)
        got_o = rep_swap[x_bit](o)
        qa, mixed = join(qa, got_a, mixed)
        got_a = rep_swap[z_bits[0]](qa)
        qb, mixed = settle(q_mine[1], q_x[1], mixed)
        got_b = rep_swap[z_bits[1]](qb)
        qa, mixed = join(qa, got_a, mixed)
        got_a = rep_swap[x_bit](qa)
        qb, mixed = join(qb, got_b, mixed)
        got_b = rep_swap[z_bits[0]](qb)
        qb, mixed = join(qb, got_b, mixed)
        got_b = rep_swap[x_bit](qb)

        def own_half(mine, got, h):
            return pick(mine, got, x ^ h)

        def blocks(total, n, of):
            return total

        rz = 2 * z_at[0] + z_at[1]
        gd_where, gd_moves, gd_in = [], [], []
        m_pairs = [(m0, got0), (m1, got1)]
        n = quarter // 2
        gd = jnp.zeros((ffq, width), F32)
        pieces = []
        for k in range(parts):
            for h in (0, 1):
                a = own_half(*m_pairs[k], h)
                pieces += [lax.dynamic_slice_in_dim(a, (b ^ rz) * n, n, 0) for b in (0, 1)]
        gd = up32(jnp.concatenate(pieces, 0))

        def u_rows(k, h):
            a = own_half(*m_pairs[k], h)
            return jnp.concatenate(
                [lax.dynamic_slice_in_dim(a, (b ^ rz) * n, n, 0) for b in (2, 3)], 0)

        theirs = [core_swap(u_rows(k, 1)) for k in range(parts)]
        mine = [u_rows(k, 0) for k in range(parts)]
        where = [0] + [(shard ^ j) * ffq + k * fp for k in range(parts) for j in range(4)]
        moves = []
        for k in range(parts):
            moves += [(k, 0, 0, fp, (0, 1 + 4 * k)), (k, 0, fp, fp, (0, 1 + 4 * k + 2)),
                      (parts + k, 0, 0, fp, (0, 1 + 4 * k + 1)),
                      (parts + k, 0, fp, fp, (0, 1 + 4 * k + 3))]
        gu = place(where, mine + theirs, (0, quarter), (quarter, ff), moves)

        def in_order(mine, got, h):
            a = own_half(mine, got, h)
            n = a.shape[0] // 4
            return jnp.concatenate(
                [lax.dynamic_slice_in_dim(a, (b ^ rz) * n, n, 0) for b in range(4)], 0)

        go = up32(jnp.concatenate([in_order(o, got_o, 0), in_order(o, got_o, 1)], 0))
        theirs = [core_swap(in_order(v, g, 1)) for v, g in ((qa, got_a), (qb, got_b))]
        mine = [in_order(v, g, 0) for v, g in ((qa, got_a), (qb, got_b))]
        where = [0] + qkv_starts(shard) + qkv_starts(shard ^ 1)
        moves = []
        for i, v in enumerate((0, 1, 2, 3)):
            for g in range(3 * pairs):
                moves.append((i, 0, g * PAIR, PAIR, (0, 1 + i * 3 * pairs + g)))
        gq = place(where, mine + theirs, (0, quarter), (quarter, 3 * width), moves)

        vectors = vectors + vec_got
        for b in rest:
            vectors = vectors + rep_swap[b](vectors)
        outs = []
        at = 0
        for size in sizes:
            outs.append(vectors[at:at + size])
            at += size
        return (
            mixed, token_grad, outs[0], outs[1], gq, outs[2], go, outs[3],
            outs[4], outs[5], gu, outs[6], gd, outs[7],
        )

    return per_device


def solution(mesh):
    rows = P(("rep", "shard"), None, None)
    vec, mat = P("shard"), P("shard", None)
    return jax.shard_map(
        build(mesh),
        mesh=mesh,
        in_specs=(rows, rows, P(("rep", "shard")), vec, vec, mat, vec, mat, vec, vec, vec,
                  mat, vec, mat, vec),
        out_specs=(rows, rows, vec, vec, mat, vec, mat, vec, vec, vec, mat, vec, mat, vec),
        check_vma=False,
    )
```

```python
import functools
import math

import jax
import jax.numpy as jnp
from jax import lax
from jax.experimental import pallas as pl
from jax.experimental.pallas import tpu as pltpu
from jax.sharding import PartitionSpec as P

HEAD_DIM = 64
PAIR = 2 * HEAD_DIM
EPSILON = 1e-06
BF = jnp.bfloat16
F32 = jnp.float32
NT = ((1,), (1,))
TN = ((0,), (0,))
VMEM_BYTES = 32 << 20


def up32(values):
    return values.astype(F32)


def flip(axis, size, bit):
    pairs = [(i, i ^ bit) for i in range(size)]
    return lambda values: lax.ppermute(values, axis, pairs)


def pick(first, second, index):
    return jnp.where(index == 0, first, second)


def dot(left, right, contract=((1,), (0,))):
    return lax.dot_general(left, right, (contract, ((), ())), preferred_element_type=F32)


def tie(*values):
    return lax.optimization_barrier(values)


def normalize(values):
    average = jnp.mean(values, -1, keepdims=True)
    centered = values - average
    inverse = lax.rsqrt(jnp.mean(centered * centered, -1, keepdims=True) + EPSILON)
    return centered * inverse, inverse


def norm_back(upstream, normed, inverse, gain):
    scaled = upstream * gain
    return inverse * (
        scaled
        - jnp.mean(scaled, -1, keepdims=True)
        - normed * jnp.mean(scaled * normed, -1, keepdims=True)
    )


def gelu_parts(values):
    phi = 0.5 * (1.0 + lax.erf(values * (1.0 / math.sqrt(2.0))))
    slope = phi + values * jnp.exp(-0.5 * values * values) * (1.0 / math.sqrt(2.0 * math.pi))
    return values * phi, slope


def attend_kernel(seq, tile, raw_ref, out_ref, log_ref):
    n = raw_ref.shape[0]
    lane = lax.broadcasted_iota(jnp.int32, (n, PAIR), 1)
    row = lax.broadcasted_iota(jnp.int32, (n, PAIR), 0)
    keys, values = raw_ref[:, PAIR:2 * PAIR], raw_ref[:, 2 * PAIR:]
    one, zero = jnp.asarray(1, BF), jnp.asarray(0, BF)
    low = jnp.asarray(-1e30, BF)
    mine = [(lane // HEAD_DIM) == h for h in (0, 1)]
    spare = [lane == (1 - h) * HEAD_DIM for h in (0, 1)]
    k_of = [jnp.where(mine[h], keys, jnp.where(spare[h] & (row >= seq), low, zero)) for h in (0, 1)]
    v_of = [jnp.where(mine[h], values, one) for h in (0, 1)]
    jobs = [(t, min(tile, n - t), h) for t in range(0, n, tile) for h in (0, 1)]

    def score(job):
        t, m, h = job
        q = raw_ref[t:t + m, :PAIR] * jnp.asarray(1.0 / math.sqrt(HEAD_DIM), BF)
        q = jnp.where(mine[h][t:t + m], q, jnp.where(spare[h][t:t + m], one, zero))
        return dot(q, k_of[h], NT)

    ahead = 2
    ready = [score(job) for job in jobs[:ahead]]
    for i, (t, m, h) in enumerate(jobs):
        if i + ahead < len(jobs):
            ready.append(score(jobs[i + ahead]))
        s = ready.pop(0)
        top = jnp.max(s, -1, keepdims=True)
        res = dot(jnp.exp(s - top).astype(BF), v_of[h])
        own = slice(h * HEAD_DIM, (h + 1) * HEAD_DIM)
        other = slice((1 - h) * HEAD_DIM, (2 - h) * HEAD_DIM)
        total = res[:, other]
        out_ref[t:t + m, own] = (res[:, own] / total).astype(BF)
        log_ref[t:t + m, own] = top + jnp.log(total)


def attend(raw, seq, images, padded, first, groups):
    spec = pl.BlockSpec((padded, PAIR), lambda i, g: (i, g))
    return pl.pallas_call(
        functools.partial(attend_kernel, seq, 304),
        grid=(images, groups),
        in_specs=[pl.BlockSpec((padded, 3 * PAIR), lambda i, g: (i, first + g))],
        out_specs=[spec, spec],
        out_shape=[
            jax.ShapeDtypeStruct((images * padded, groups * PAIR), BF),
            jax.ShapeDtypeStruct((images * padded, groups * PAIR), F32),
        ],
        compiler_params=pltpu.CompilerParams(vmem_limit_bytes=VMEM_BYTES),
        name="attend",
    )(raw)


def attend_back_kernel(seq, wide, raw_ref, d_ref, log_ref, out_ref, sum_ref, kk_ref, vv_ref, p_ref,
                       s_ref):
    n = raw_ref.shape[0]
    scale = 1.0 / math.sqrt(HEAD_DIM)
    lane = lax.broadcasted_iota(jnp.int32, (n, PAIR), 1)
    zero = jnp.asarray(0, BF)
    gap = jnp.zeros((wide - n, PAIR), BF)

    def stacked(v):
        first = lane < HEAD_DIM
        return jnp.concatenate([jnp.where(first, v, zero), gap, jnp.where(first, zero, v), gap], 0)

    kk_ref[:, :PAIR] = stacked(raw_ref[:, PAIR:2 * PAIR])
    vv_ref[...] = stacked(raw_ref[:, 2 * PAIR:])

    @pl.when((pl.program_id(0) == 0) & (pl.program_id(1) == 0))
    def _():
        lanes = lax.broadcasted_iota(jnp.int32, (2 * wide, PAIR), 1)
        row = lax.broadcasted_iota(jnp.int32, (2 * wide, PAIR), 0)
        row = jnp.where(row >= wide, row - wide, row)
        kk_ref[:, PAIR:] = jnp.where((lanes == 0) & (row >= seq), jnp.asarray(-1e30, BF), zero)

    q = raw_ref[:, :PAIR]
    d = d_ref[...]
    mask = jnp.where(lane == 0, jnp.asarray(1, BF), zero)
    s = dot(jnp.concatenate([q * jnp.asarray(scale, BF), mask], 1), kk_ref[...], NT)
    dp = dot(d, vv_ref[...], NT)
    for h in (0, 1):
        cols = slice(h * wide, (h + 1) * wide)
        p = jnp.exp(s[:, cols] - log_ref[:, h * HEAD_DIM:h * HEAD_DIM + 1])
        dph = dp[:, cols]
        p_ref[:, cols] = p.astype(BF)
        s_ref[:, cols] = (p * (dph - jnp.sum(dph * p, -1, keepdims=True))).astype(BF)
    dk = dot(s_ref[...], q, TN)
    dv = dot(p_ref[...], d, TN)
    first = lane < HEAD_DIM
    for j, value in enumerate((
            dot(s_ref[...], kk_ref[:, :PAIR]) * scale,
            jnp.where(first, dk[:n], dk[wide:wide + n]) * scale,
            jnp.where(first, dv[:n], dv[wide:wide + n]))):
        cols = slice(j * PAIR, (j + 1) * PAIR)
        low = value.astype(BF)
        out_ref[:, cols] = low
        sum_ref[0, :, cols] = jnp.broadcast_to(
            jnp.sum(up32(low), 0, keepdims=True), (sum_ref.shape[1], PAIR))


def attend_back(raw, d_att, logs, seq, images, padded, start, groups):
    wide = -(-padded // 128) * 128
    one = pl.BlockSpec((padded, PAIR), lambda i, g: (i, start + g))
    log = pl.BlockSpec((padded, PAIR), lambda i, g: (i, g))
    three = pl.BlockSpec((padded, 3 * PAIR), lambda i, g: (i, start + g))
    cols = groups * 3 * PAIR
    return pl.pallas_call(
        functools.partial(attend_back_kernel, seq, wide),
        grid=(images, groups),
        in_specs=[three, one, log],
        out_specs=[pl.BlockSpec((padded, 3 * PAIR), lambda i, g: (i, g)),
                   pl.BlockSpec((1, 8, 3 * PAIR), lambda i, g: (i, 0, g))],
        out_shape=[jax.ShapeDtypeStruct((raw.shape[0], cols), BF),
                   jax.ShapeDtypeStruct((images, 8, cols), F32)],
        scratch_shapes=[
            pltpu.VMEM((2 * wide, 2 * PAIR), BF),
            pltpu.VMEM((2 * wide, PAIR), BF),
            pltpu.VMEM((padded, 2 * wide), BF),
            pltpu.VMEM((padded, 2 * wide), BF),
        ],
        compiler_params=pltpu.CompilerParams(vmem_limit_bytes=VMEM_BYTES),
        name="attend_back",
    )(raw, d_att, logs)


TILE = 304


def whole(array):
    return pl.BlockSpec(array.shape, lambda *_: (0,) * array.ndim)


def params():
    return pltpu.CompilerParams(vmem_limit_bytes=VMEM_BYTES)


def spread_kernel(size, starts, w_ref, out_ref):
    rows = w_ref.shape[0]
    wide = out_ref.shape[1] // size
    for i, start in enumerate(starts):
        row, col = i // wide * rows, i % wide * size
        out_ref[row:row + rows, col:col + size] = w_ref[:, start:start + size]


def spread(w, starts, size, blocks):
    out = jax.ShapeDtypeStruct((w.shape[0] * blocks, len(starts) // blocks * size), w.dtype)
    return pl.pallas_call(
        functools.partial(spread_kernel, size, starts), grid=(1,), in_specs=[whole(w)],
        out_specs=whole(out), out_shape=out, compiler_params=params(), name="spread")(w)


def row_mask(tile, seq):
    return lax.broadcasted_iota(jnp.int32, (TILE, 1), 0) + tile * TILE < seq


def near_first(value, y):
    half = value.shape[1] // 2
    a, b = value[:, :half], value[:, half:]
    return jnp.concatenate([jnp.where(y == 0, a, b), jnp.where(y == 0, b, a)], 1)


def column_sum(value):
    return jnp.sum(value, 0, keepdims=True)


def rows_call(kernel, scalars, arrays, vectors, outs, sums, name):
    images = arrays[-1].shape[-3]
    padded = max(v.shape[-2] for v in (*arrays, *outs))

    def spec(v):
        if len(v.shape) == 3:
            return pl.BlockSpec((1, TILE, v.shape[-1]), lambda i, t, s: (i, t, 0))
        return pl.BlockSpec((2, 1, TILE, v.shape[-1]), lambda i, t, s: (0, i, t, 0))

    width = arrays[0].shape[-1]
    more = [jax.ShapeDtypeStruct((8, width), F32)] if sums else []
    return pl.pallas_call(
        kernel,
        grid_spec=pltpu.PrefetchScalarGridSpec(
            num_scalar_prefetch=1, grid=(images, -(-padded // TILE)),
            in_specs=[*map(spec, arrays), *map(whole, vectors)],
            out_specs=[*map(spec, outs), *map(whole, more)]),
        out_shape=[*outs, *more],
        compiler_params=params(),
        name=name,
    )(scalars, *arrays, *vectors)


def enter_kernel(seq, s_ref, x_ref, grad_ref, gain_ref, shift_ref, norm_ref, out_ref):
    i = pl.program_id(0)
    ok = row_mask(pl.program_id(1), seq)
    unit, _ = normalize(up32(x_ref[0]))
    normed = jnp.where(ok, near_first(unit * gain_ref[...] + shift_ref[...], s_ref[0]), 0.0)
    valid = s_ref[1 + i]
    grad = jnp.where(ok & (valid != 0), up32(grad_ref[0]) * up32(valid), 0.0)
    for k in (0, 1):
        norm_ref[k, 0] = normed.astype(BF)
        out_ref[k, 0] = grad.astype(BF)


def middle_kernel(seq, s_ref, x_ref, parts_ref, add_ref, gain_ref, shift_ref, mid_ref, norm_ref):
    ok = row_mask(pl.program_id(1), seq)
    middle = up32(x_ref[0]) + (up32(parts_ref[0, 0]) + up32(parts_ref[1, 0])) + add_ref[...]
    middle = jnp.where(ok, middle, 0.0)
    mid_ref[0] = middle
    unit, _ = normalize(middle)
    normed = jnp.where(ok, near_first(unit * gain_ref[...] + shift_ref[...], s_ref[0]), 0.0)
    for k in (0, 1):
        norm_ref[k, 0] = normed.astype(BF)


def mixed_kernel(seq, s_ref, parts_ref, mid_ref, add_ref, out_ref):
    parts = up32(parts_ref[0, 0]) + up32(parts_ref[1, 0])
    out_ref[0] = (mid_ref[0] + parts + add_ref[...]).astype(BF)


def start_sums(sum_ref):
    @pl.when((pl.program_id(0) == 0) & (pl.program_id(1) == 0))
    def _():
        sum_ref[...] = jnp.zeros_like(sum_ref)


def back_middle_kernel(seq, s_ref, parts_ref, mid_ref, grad_ref, gain_ref, d_ref, low_ref, sum_ref):
    i = pl.program_id(0)
    ok = row_mask(pl.program_id(1), seq)
    unit, inverse = normalize(mid_ref[0])
    h = near_first(up32(parts_ref[0, 0]) + up32(parts_ref[1, 0]), s_ref[0])
    h = jnp.where(ok, h, 0.0)
    unit = jnp.where(ok, unit, 0.0)
    valid = s_ref[1 + i]
    dy = jnp.where(ok & (valid != 0), up32(grad_ref[0]) * up32(valid), 0.0)
    d_middle = jnp.where(ok, dy + norm_back(h, unit, inverse, gain_ref[...]), 0.0)
    low = d_middle.astype(BF)
    d_ref[0] = d_middle
    for k in (0, 1):
        low_ref[k, 0] = low
    start_sums(sum_ref)
    for row, value in enumerate((h * unit, h, up32(low), up32(dy.astype(BF)))):
        sum_ref[row:row + 1, :] += column_sum(value)


def leave_kernel(seq, s_ref, parts_ref, x_ref, mid_ref, gain_ref, d_ref, sum_ref):
    ok = row_mask(pl.program_id(1), seq)
    unit, inverse = normalize(up32(x_ref[0]))
    h = near_first(up32(parts_ref[0, 0]) + up32(parts_ref[1, 0]), s_ref[0])
    h = jnp.where(ok, h, 0.0)
    d_ref[0] = (mid_ref[0] + norm_back(h, unit, inverse, gain_ref[...])).astype(BF)
    start_sums(sum_ref)
    for row, value in enumerate((jnp.where(ok, h * unit, 0.0), h)):
        sum_ref[row:row + 1, :] += column_sum(value)


def place_kernel(count, moves, where_ref, *refs):
    ins, out_ref = refs[:count], refs[count]
    for number, col, size, entry in moves:
        start = pl.multiple_of(where_ref[entry], 128)
        out_ref[:, pl.ds(start, size)] = up32(ins[number][:, col:col + size])


def place(where, inputs, width, moves):
    out = jax.ShapeDtypeStruct((inputs[0].shape[0], width), F32)
    return pl.pallas_call(
        functools.partial(place_kernel, len(inputs), moves),
        grid_spec=pltpu.PrefetchScalarGridSpec(
            num_scalar_prefetch=1, grid=(1,), in_specs=[whole(v) for v in inputs],
            out_specs=whole(out)),
        out_shape=out,
        compiler_params=params(),
        name="place",
    )(jnp.stack([jnp.asarray(w, jnp.int32) for w in where]), *inputs)


def pack_kernel(*refs):
    at = 0
    for ref in refs[:-1]:
        refs[-1][:, at:at + ref.shape[1]] = up32(ref[...])
        at += ref.shape[1]


def pack(*vectors):
    vectors = [v[None] for v in vectors]
    out = jax.ShapeDtypeStruct((1, sum(v.shape[1] for v in vectors)), F32)
    return pl.pallas_call(
        pack_kernel, grid=(1,), in_specs=[whole(v) for v in vectors], out_specs=whole(out),
        out_shape=out, compiler_params=params(), name="pack")(*vectors)


def small_kernel(offsets, quarter, parts, pairs, c_ref, all_ref, vec_ref, bias_ref, upb_ref):
    c = c_ref[0]

    def of(shard, start, size):
        row = shard % 2 * 2 + shard // 2
        return all_ref[row:row + 1, start:start + size]

    for row, at in enumerate(offsets[:6]):
        for q in range(4):
            vec_ref[row:row + 1, q * quarter:(q + 1) * quarter] = of(q, at, quarter)
    qv, up = offsets[6:]

    def block(b):
        return of(b // 2, qv + b % 2 * quarter, quarter)

    for side in (0, 1):
        for part in range(3):
            if part == 1:
                value = jnp.zeros((1, quarter), F32)
            else:
                b = 2 * part + 2 * side
                value = jnp.where(c == 0, block(b), block(b + 1))
            for g in range(pairs):
                to = ((side * pairs + g) * 3 + part) * PAIR
                bias_ref[:, to:to + PAIR] = value[:, g * PAIR:(g + 1) * PAIR]
    fp = upb_ref.shape[1] // 2 // parts
    for k in range(parts):
        for side in (0, 1):
            to = (2 * k + side) * fp
            start = up + k * fp
            upb_ref[:, to:to + fp] = jnp.where(
                c == 0, of(2 * side, start, fp), of(2 * side + 1, start, fp))


def small_call(core, gathered, offsets, quarter, ffq, parts, pairs):
    shapes = [jax.ShapeDtypeStruct(s, F32)
              for s in ((8, 4 * quarter), (1, 6 * quarter), (1, 2 * ffq))]
    return pl.pallas_call(
        functools.partial(small_kernel, offsets, quarter, parts, pairs),
        grid_spec=pltpu.PrefetchScalarGridSpec(
            num_scalar_prefetch=1, grid=(1,), in_specs=[whole(gathered)],
            out_specs=[whole(s) for s in shapes]),
        out_shape=shapes,
        compiler_params=params(),
        name="small",
    )(core, gathered)


def vectors_kernel(offsets, quarter, parts, pairs, c_ref, one_ref, two_ref, low_ref, high_ref, *refs):
    ups, out_ref = refs[:parts], refs[parts]
    c = c_ref[0]
    rows = ((one_ref, 0), (one_ref, 1), (two_ref, 2), (two_ref, 0), (two_ref, 1), (two_ref, 3))
    qv, up = offsets[6:]

    def sums(ref, part):
        total = jnp.sum(ref[:, 0, :], 0, keepdims=True)
        return jnp.concatenate(
            [total[:, (3 * g + part) * PAIR:(3 * g + part + 1) * PAIR] for g in range(pairs)], 1)

    table = [[sums(ref, part) for part in (0, 2)] for ref in (low_ref, high_ref)]
    fp = ups[0].shape[1] // 2
    for core in (0, 1):
        for side in (0, 1):
            to = 2 * core + side
            shard = 2 * side + core
            for (ref, row), at in zip(rows, offsets[:6]):
                out_ref[to:to + 1, at:at + quarter] = (
                    ref[row:row + 1, shard * quarter:(shard + 1) * quarter])
            for h in (0, 1):
                block = 2 * shard + h
                value = table[block % 4 // 2][block // 4]
                out_ref[to:to + 1, qv + h * quarter:qv + (h + 1) * quarter] = jnp.where(
                    c == block % 2, value, 0.0)
            for k, ref in enumerate(ups):
                out_ref[to:to + 1, up + k * fp:up + (k + 1) * fp] = jnp.where(
                    c == core, ref[:, side * fp:(side + 1) * fp], 0.0)


def vectors_call(core, one, two, low, high, ups, offsets, quarter, width, pairs):
    out = jax.ShapeDtypeStruct((4, width), F32)
    ins = [one, two, low, high, *ups]
    return pl.pallas_call(
        functools.partial(vectors_kernel, offsets, quarter, len(ups), pairs),
        grid_spec=pltpu.PrefetchScalarGridSpec(
            num_scalar_prefetch=1, grid=(1,), in_specs=[whole(v) for v in ins],
            out_specs=whole(out)),
        out_shape=out,
        compiler_params=params(),
        name="vectors",
    )(core, *ins)


def feed_kernel(s_ref, n2_ref, do_ref, own_ref, other_ref, ua_ref, ub_ref, near_ref, da_ref,
                db_ref, bias_ref, h_ref, act_ref, keep_ref, send_ref, hsum_ref,
                sum_ref, up_ref, down_ref, acc_ref):
    x, y = s_ref[0], s_ref[1]
    j = pl.program_id(0)
    steps = pl.num_programs(0)
    half = steps // 2
    wide = up_ref.shape[1]
    quarter = own_ref.shape[0]
    up_ref[:quarter, :] = own_ref[...]
    up_ref[quarter:2 * quarter, :] = other_ref[...]
    a, b = ua_ref[...], ub_ref[...]
    up_ref[2 * quarter:3 * quarter, :] = jnp.where(x == 0, a, b)
    up_ref[3 * quarter:, :] = jnp.where(x == 0, b, a)
    near = j // half == y

    @pl.when(near)
    def _():
        down_ref[...] = near_ref[...]

    @pl.when(jnp.logical_not(near))
    def _():
        down_ref[...] = jnp.where((x == 0) == (j % half == 0), da_ref[...], db_ref[...])

    n2, do = n2_ref[...], do_ref[...]
    act, slope = gelu_parts(dot(n2, up_ref[...]) + bias_ref[...])
    act = act.astype(BF)
    act_ref[...] = act
    d_pre = (dot(do, down_ref[...], NT) * slope).astype(BF)
    sum_ref[...] = jnp.sum(up32(d_pre), 0, keepdims=True)
    gd = dot(act, do, TN).astype(BF)
    at_rows = pl.ds(pl.multiple_of(j % half * wide, wide), wide)

    @pl.when(near)
    def _():
        keep_ref[at_rows, :] = gd

    @pl.when(jnp.logical_not(near))
    def _():
        send_ref[at_rows, :] = gd

    gu = dot(n2, d_pre, TN).astype(BF)
    cols = pl.ds(pl.multiple_of(j * wide, wide), wide)
    keep_ref[half * wide:, cols] = gu[:2 * quarter]
    send_ref[half * wide:, cols] = gu[2 * quarter:]

    @pl.when(j == 0)
    def _():
        acc_ref[...] = h_ref[...]

    acc_ref[...] += dot(d_pre, up_ref[...], NT)

    @pl.when(j == steps - 1)
    def _():
        hsum_ref[...] = acc_ref[...].astype(BF)


def feed(scalars, n2, do, near_up, a, b, down, bias, h, k, wide=256):
    both, width = n2.shape
    quarter = width // 4
    cols = bias.shape[1]
    half = cols // 2 // wide
    parts = near_up.shape[0] // 2 // quarter
    n2_spec = whole(n2)
    piece = jax.ShapeDtypeStruct((cols // 2 + width // 2, width), BF)
    low = jax.ShapeDtypeStruct((both, width), BF)

    def near(j, s):
        return (k * half + jnp.where(j // half == s[1], j % half, 0), 0)

    return pl.pallas_call(
        feed_kernel,
        grid_spec=pltpu.PrefetchScalarGridSpec(
            num_scalar_prefetch=1, grid=(2 * half,),
            in_specs=[
                n2_spec, n2_spec,
                pl.BlockSpec((quarter, wide), lambda j, s: (k, j)),
                pl.BlockSpec((quarter, wide), lambda j, s: (parts + k, j)),
                pl.BlockSpec((quarter, wide), lambda j, s: (0, j)),
                pl.BlockSpec((quarter, wide), lambda j, s: (0, j)),
                pl.BlockSpec((wide, width), near),
                pl.BlockSpec((wide, width), lambda j, s: (quarter // wide, 0)),
                pl.BlockSpec((wide, width), lambda j, s: (quarter // wide, 0)),
                pl.BlockSpec((1, wide), lambda j, s: (0, j)),
                whole(h)],
            out_specs=[
                pl.BlockSpec((both, wide), lambda j, s: (0, j)),
                whole(piece), whole(piece),
                whole(low),
                pl.BlockSpec((1, wide), lambda j, s: (0, j))],
            scratch_shapes=[pltpu.VMEM((width, wide), BF), pltpu.VMEM((wide, width), BF),
                            pltpu.VMEM((both, width), F32)]),
        out_shape=[jax.ShapeDtypeStruct((both, cols), BF), piece, piece, low,
                   jax.ShapeDtypeStruct((1, cols), F32)],
        compiler_params=pltpu.CompilerParams(vmem_limit_bytes=58 << 20),
        name="feed",
    )(scalars, n2, do, near_up, near_up, a, b, down, a, b, bias, h)


def halve_kernel(sizes, s_ref, keep_ref, got_ref, mine_ref, theirs_ref):
    at = 0
    for i, size in enumerate(sizes):
        n = size // 2
        for bit, out_ref in ((s_ref[i], mine_ref), (1 - s_ref[i], theirs_ref)):
            rows = pl.ds(pl.multiple_of(at + bit * n, 16), n)
            out_ref[at // 2:at // 2 + n, :] = added(keep_ref[rows, :], got_ref[rows, :])
        at += size


def add_kernel(keep_ref, got_ref, out_ref):
    out_ref[...] = added(keep_ref[...], got_ref[...])


def pick_kernel(sizes, cross, s_ref, keep_ref, got_ref, out_ref):
    at = 0
    for size, crosses in zip(sizes, cross):
        rows = slice(at, at + size)
        keep = keep_ref[rows, :]
        out_ref[rows, :] = jnp.where(s_ref[0] == 0, keep, got_ref[rows, :]) if crosses else keep
        at += size


def join_kernel(sizes, s_ref, keep_ref, got_ref, out_ref):
    at = 0
    for size in sizes:
        rows = slice(at, at + size)
        keep, got = keep_ref[rows, :], got_ref[rows, :]
        out_ref[2 * at:2 * at + size, :] = jnp.where(s_ref[0] == 0, keep, got)
        out_ref[2 * at + size:2 * (at + size), :] = jnp.where(s_ref[0] == 0, got, keep)
        at += size


def columns_call(kernel, scalars, arrays, rows, block, outs, name):
    width = 256
    spec = pl.BlockSpec((rows, width), lambda j, *_: (block, j))
    out_specs = [pl.BlockSpec((n, width), lambda j, *_: (0, j)) for n in outs]
    cols = arrays[0].shape[1]
    return pl.pallas_call(
        kernel,
        grid_spec=pltpu.PrefetchScalarGridSpec(
            num_scalar_prefetch=len(scalars), grid=(cols // width,),
            in_specs=[spec] * len(arrays), out_specs=out_specs),
        out_shape=[jax.ShapeDtypeStruct((n, cols), BF) for n in outs],
        compiler_params=params(),
        name=name,
    )(*scalars, *arrays)


def pair_kernel(n_ref, a_ref, b_ref, out_ref):
    for j, ref in enumerate((a_ref, b_ref)):
        @pl.when(pl.program_id(0) == j)
        def _(ref=ref):
            out_ref[...] = dot(n_ref[...], ref[...], TN).astype(BF)


def pair_sums(n, a, b, side):
    rows, half = n.shape[0], n.shape[1] // 2
    cols = a.shape[1]
    return pl.pallas_call(
        pair_kernel,
        grid=(2,),
        in_specs=[pl.BlockSpec((rows, half), lambda j: (0, side)), whole(a), whole(b)],
        out_specs=pl.BlockSpec((half, cols), lambda j: (j, 0)),
        out_shape=jax.ShapeDtypeStruct((2 * half, cols), BF),
        compiler_params=params(),
        name="pair_sums",
    )(n, a, b)


def back_in_kernel(a_ref, b_ref, w_ref, out_ref):
    cut = a_ref.shape[1]
    total = dot(a_ref[...], w_ref[:, :cut], NT) + dot(b_ref[...], w_ref[:, cut:], NT)
    out_ref[...] = total.astype(BF)


def back_in(a, b, w, wide=512):
    out = jax.ShapeDtypeStruct((a.shape[0], w.shape[0]), BF)
    return pl.pallas_call(
        back_in_kernel,
        grid=(w.shape[0] // wide,),
        in_specs=[whole(a), whole(b), pl.BlockSpec((wide, w.shape[1]), lambda j: (j, 0))],
        out_specs=pl.BlockSpec((a.shape[0], wide), lambda j: (0, j)),
        out_shape=out,
        compiler_params=params(),
        name="back_in",
    )(a, b, w)


def out_sums_kernel(s_ref, a_ref, b_ref, d_ref, send_ref, keep_ref):
    d = d_ref[...]
    for j, out_ref in enumerate((send_ref, keep_ref)):
        for y, ref in enumerate((a_ref, b_ref)):
            @pl.when((pl.program_id(0) == j) & (s_ref[0] == (y ^ 1 ^ j)))
            def _(ref=ref, out_ref=out_ref):
                out_ref[...] = dot(ref[...], d, TN).astype(BF)


def out_sums(scalars, a, b, d):
    out = jax.ShapeDtypeStruct((a.shape[1], d.shape[1]), BF)
    return pl.pallas_call(
        out_sums_kernel,
        grid_spec=pltpu.PrefetchScalarGridSpec(
            num_scalar_prefetch=1, grid=(2,), in_specs=[whole(a), whole(b), whole(d)],
            out_specs=[whole(out)] * 2),
        out_shape=[out] * 2,
        compiler_params=params(),
        name="out_sums",
    )(scalars, a, b, d)


def feed_out_kernel(s_ref, one_ref, two_ref, down_ref, near_ref, a_ref, b_ref, out_ref):
    x, y = s_ref[0], s_ref[1]
    n = near_ref.shape[0]
    total = dot(one_ref[...], down_ref[...])
    total += dot(two_ref[:, pl.ds(pl.multiple_of(y * n, n), n)], near_ref[...])
    a, b = a_ref[...], b_ref[...]
    for i, w in enumerate((jnp.where(x == 0, a, b), jnp.where(x == 0, b, a))):
        start = pl.multiple_of((1 - y) * n + i * (n // 2), n // 2)
        total += dot(two_ref[:, pl.ds(start, n // 2)], w)
    out_ref[...] = total.astype(BF)


def feed_out(scalars, one, two, down, near, a, b, k, wide=512):
    rows, cols = one.shape[0], down.shape[1]
    n = two.shape[1] // 2
    return pl.pallas_call(
        feed_out_kernel,
        grid_spec=pltpu.PrefetchScalarGridSpec(
            num_scalar_prefetch=1, grid=(cols // wide,),
            in_specs=[
                whole(one), whole(two), pl.BlockSpec((down.shape[0], wide), lambda j, s: (0, j)),
                pl.BlockSpec((n, wide), lambda j, s: (k, j)),
                pl.BlockSpec((n // 2, wide), lambda j, s: (1, j)),
                pl.BlockSpec((n // 2, wide), lambda j, s: (1, j))],
            out_specs=pl.BlockSpec((rows, wide), lambda j, s: (0, j))),
        out_shape=jax.ShapeDtypeStruct((rows, cols), BF),
        compiler_params=params(),
        name="feed_out",
    )(scalars, one, two, down, near, a, b)


class Line:
    def __init__(self, token):
        self.token = token

    def tie(self, *values):
        *values, self.token = lax.optimization_barrier((*values, self.token))
        return values[0] if len(values) == 1 else values

    def do(self, step, *values):
        values = self.tie(*values)
        out = step(*values) if isinstance(values, list) else step(values)
        return self.tie(*out) if isinstance(out, (list, tuple)) else self.tie(out)


def added(keep, got):
    return (up32(keep) + up32(got)).astype(BF)


class Sum:
    def __init__(self, line, swaps, at, got, keep, sizes, cross, block=0):
        self.line, self.swaps, self.at, self.cross = line, swaps, at, cross
        self.got, self.keep, self.sizes, self.block = got, keep, sizes, block

    def run(self, kernel, bits, outs, name):
        scalars = [jnp.stack(bits).astype(jnp.int32)] if bits else []
        out = self.line.do(
            lambda keep, got: columns_call(
                kernel, scalars, [keep, got], sum(self.sizes), self.block, outs, name),
            self.keep, self.got)
        self.block = 0
        return out

    def halve(self, axis):
        bits = [self.at["cross" if cross and axis == "x" else axis] for cross in self.cross]
        n = sum(self.sizes) // 2
        self.keep, theirs = self.run(
            functools.partial(halve_kernel, self.sizes), bits, [n, n], "halve")
        self.sizes = [n // 2 for n in self.sizes]
        self.got = self.swaps[axis](theirs)

    def add(self):
        self.keep = self.run(add_kernel, [], [sum(self.sizes)], "add")

    def exchange(self, axis):
        self.add()
        self.got = self.swaps[axis](self.keep)

    def back(self):
        self.add()
        for swap in self.swaps["rest"]:
            self.got = swap(self.keep)
            self.add()
        if any(self.cross):
            self.got = self.swaps["core"](self.keep)
            self.keep = self.run(
                functools.partial(pick_kernel, self.sizes, self.cross), [self.at["x"]],
                [sum(self.sizes)], "pick")
        self.got = self.swaps["z1"](self.keep)

    def join(self):
        self.keep = self.run(
            functools.partial(join_kernel, self.sizes), [self.at["z1"]], [2 * sum(self.sizes)], "join")
        self.sizes = [2 * n for n in self.sizes]
        self.got = self.swaps["x"](self.keep)

    def land(self):
        self.got = self.line.tie(self.got)

    def ends(self):
        at, out = 0, []
        for n in self.sizes:
            keep, got = self.keep[at:at + n], self.got[at:at + n]
            at += n
            out += [pick(keep, got, self.at["x"]), pick(got, keep, self.at["x"])]
        return out


def build(mesh):
    reps = mesh.shape["rep"]
    shards = mesh.shape["shard"]
    y_swap = flip("shard", shards, 2)
    cores = [[2 * i, 2 * i + 1] for i in range(shards // 2)]
    bits = [1 << i for i in range(reps.bit_length() - 1)]
    rep_swap = {b: flip("rep", reps, b) for b in bits}

    def core_swap(values):
        return lax.all_to_all(values, "shard", 0, 0, axis_index_groups=cores, tiled=True)

    swaps = {"core": flip("shard", shards, 1), "y": y_swap, "x": rep_swap[bits[0]], "z1": rep_swap[bits[1]],
             "z2": rep_swap[bits[2]], "rest": [rep_swap[b] for b in bits[3:]]}

    def per_device(
        tokens, out_grad, valid, attn_gain, attn_shift, qkv_w, qv_b, out_w, out_b,
        mlp_gain, mlp_shift, up_w, up_b, down_w, down_b,
    ):
        images, seq, width = tokens.shape
        ff = up_w.shape[1]
        quarter = width // shards
        half = width // 2
        ffq = ff // shards
        padded = -(-seq // 16) * 16
        rows = images * padded
        shard = lax.axis_index("shard")
        rep = lax.axis_index("rep")
        y, c = shard // 2, shard % 2
        x = rep % 2
        at = {"x": x, "z1": (rep // 2) % 2, "z2": (rep // 4) % 2, "cross": x ^ c}
        pairs = quarter // PAIR
        parts = 2
        fp = ffq // parts
        core = c[None].astype(jnp.int32)
        scalars = jnp.concatenate([y[None], valid]).astype(jnp.int32)
        place_at = jnp.stack([x, y]).astype(jnp.int32)

        def qkv_starts(core):
            return [part * width + (2 * side + core) * quarter + g * PAIR
                    for side in (0, 1) for g in range(pairs) for part in range(3)]

        def up_starts(core):
            return [(2 * side + core) * ffq + k * fp for k in range(parts) for side in (0, 1)]

        def by_x(v):
            n = v.shape[0] // 2
            return lax.dynamic_slice_in_dim(v, x * n, n, 0)

        def in_order(got, swapped):
            return [pick(got, swapped, x), pick(swapped, got, x)]

        line = Line(valid)
        near_qkv = line.do(lambda w: spread(w, qkv_starts(0) + qkv_starts(1), PAIR, 2), qkv_w)
        near_qkv = line.do(core_swap, near_qkv)
        far = y_swap(line.do(by_x, near_qkv))
        small = line.do(pack, attn_gain, attn_shift, out_b, mlp_gain, mlp_shift, down_b, qv_b, up_b)
        offsets = [i * quarter for i in range(7)] + [8 * quarter]
        far_small = y_swap(small)
        near_up = line.do(
            lambda w: spread(w, up_starts(0) + up_starts(1), fp, 2 * parts), up_w)
        near_up = line.do(core_swap, near_up)
        out_w = line.tie(out_w)
        far_out = y_swap(out_w)

        def far_part(k):
            def step(a, w):
                at = (parts * x + k) * quarter
                return jnp.concatenate([
                    lax.dynamic_slice_in_dim(a, at, quarter, 0), by_x(w[k * fp:(k + 1) * fp])], 0)

            return y_swap(line.do(step, near_up, down_w))

        far_mlp, far_mlp2 = [far_part(0)], []
        far = line.tie(far)
        far2 = swaps["x"](far)
        small = line.do(
            lambda a, b: jnp.concatenate([pick(a, b, y), pick(b, a, y)] * 2, 0), small, far_small)
        small = line.do(core_swap, small)
        vec, bias, upb = line.do(
            lambda v: small_call(core, v, offsets, quarter, ffq, parts, pairs), small)
        g1, b1, ob, g2, b2, db = [vec[i:i + 1] for i in range(6)]

        def shaped(dtype, *lead):
            return jax.ShapeDtypeStruct((*lead, images, padded, width), dtype)

        def cube(v):
            return v.reshape(2, images, padded, width)

        def flat(v):
            return v.reshape(2 * rows, width)

        def kernel(body):
            return functools.partial(body, seq)

        normed1, d_out = line.do(
            lambda a, b, g, s: rows_call(
                kernel(enter_kernel), scalars, [a, b], [g, s], [shaped(BF, 2)] * 2, False, "enter"),
            tokens, out_grad, g1, b1)
        far_mlp.append(far_part(1))
        normed1 = line.do(core_swap, flat(normed1))
        d_out = line.do(core_swap, flat(d_out))
        far2 = line.tie(far2)
        qkv_full = line.do(
            lambda a, b, d: jnp.concatenate([a, *in_order(b, d)], 0), near_qkv, far, far2)
        raw = line.do(
            lambda n, w, b: (dot(n, w) + b).astype(BF), normed1, qkv_full, bias)
        far_out = line.tie(far_out)

        def attention(first):
            return line.do(lambda v: attend(v, seq, 2 * images, padded, first, pairs), raw)

        def by_y(near, far):
            return [pick(near, far, y), pick(far, near, y)]

        attended, logs = [None] * 2, [None] * 2
        attended[0], logs[0] = attention(0)
        out_full = line.do(lambda a, b: jnp.concatenate(by_y(a, b), 0), out_w, far_out)
        far_mlp[0] = line.tie(far_mlp[0])
        far_mlp2.append(swaps["x"](far_mlp[0]))
        attended[1], logs[1] = attention(pairs)
        branch = line.do(
            lambda a, b, w: (dot(a, w[:quarter]) + dot(b, w[quarter:])).astype(BF),
            *attended, out_full)
        branch = line.do(core_swap, branch)
        middle, normed2 = line.do(
            lambda a, p, *v: rows_call(
                kernel(middle_kernel), scalars, [a, cube(p)], v, [shaped(F32), shaped(BF, 2)],
                False, "middle"),
            tokens, branch, ob, g2, b2)
        normed2 = line.do(core_swap, flat(normed2))
        far_mlp[1] = line.tie(far_mlp[1])
        far_mlp2.append(swaps["x"](far_mlp[1]))

        def tn(a, b):
            return dot(a, b, TN).astype(BF)

        def of_y(v):
            n = v.shape[0] // 2
            return [lax.dynamic_slice_in_dim(v, side * n, n, 0) for side in (1 - y, y)]

        def start(got, keep, sizes, cross, block=0):
            return Sum(line, swaps, at, got, keep, sizes, cross, block)

        n = fp // 2

        def whole_up(a, b, d):
            return jnp.concatenate(
                [a[:quarter], a[parts * quarter:(parts + 1) * quarter],
                 *in_order(b[:quarter], d[:quarter])], 0)

        def whole_down(k):
            def step(near, a, b):
                near, (a, b) = near[k * fp:(k + 1) * fp], in_order(a[quarter:], b[quarter:])
                return jnp.concatenate(
                    [pick(near[:n], a, y), pick(near[n:], b, y),
                     pick(a, near[:n], y), pick(b, near[n:], y)], 0)

            return line.do(step, down_w, far_mlp[k], far_mlp2[k])

        up = line.do(whole_up, near_up, far_mlp[0], far_mlp2[0])

        def forward(n, w, b):
            act, slope = gelu_parts(dot(n, w) + b)
            return act.astype(BF), slope

        act, slope = line.do(forward, normed2, up, upb[:, :2 * fp])
        d_send, d_keep = line.do(of_y, line.do(tn, act, d_out))
        down = whole_down(0)

        def backward(d, w, sl):
            d_pre = (dot(d, w, NT) * sl).astype(BF)
            return d_pre, jnp.sum(up32(d_pre), 0, keepdims=True)

        d_pre, up_sum = line.do(backward, d_out, down, slope)
        far_mlp2[1] = line.tie(far_mlp2[1])
        m_got = y_swap(line.do(
            lambda n, d, v: jnp.concatenate([v, tn(n[:, half:], d)], 0), normed2, d_pre, d_send))
        m_keep = line.do(
            lambda n, d, v: jnp.concatenate([v, tn(n[:, :half], d)], 0), normed2, d_pre, d_keep)
        m0 = start(m_got, m_keep, [fp, half], [False, True])
        h = line.do(lambda d, w: dot(d, w, NT), d_pre, up)
        act2, keep, send, h, up_sum2 = line.do(
            lambda *v: feed(place_at, *v, 1),
            normed2, d_out, near_up, far_mlp[1], far_mlp2[1], down_w, upb[:, 2 * fp:], h)
        m1 = start(y_swap(send), keep, [fp, half], [False, True])
        h = line.do(core_swap, h)
        d_middle, d_branch, sums2 = line.do(
            lambda p, m, d, g: rows_call(
                kernel(back_middle_kernel), scalars, [cube(p), m, d], [g],
                [shaped(F32), shaped(BF, 2)], True, "back_middle"),
            h, middle, out_grad, g2)
        d_branch = line.do(core_swap, flat(d_branch))
        m0.halve("x")
        d_att = line.do(lambda d, w: dot(d, w, NT).astype(BF), d_branch, out_full)
        def attention_back(first):
            return line.do(
                lambda a, b, c: attend_back(a, b, c, seq, 2 * images, padded, first, pairs),
                raw, d_att, logs[first // pairs])

        d_raws, col_sums = [None] * 2, [None] * 2
        d_raws[0], col_sums[0] = attention_back(0)
        d_raws[1], col_sums[1] = attention_back(pairs)
        m0.halve("z1")
        m1.halve("x")
        q_got = y_swap(line.do(lambda n, a, b: pair_sums(n, a, b, 1), normed1, *d_raws))
        q_keep = line.do(lambda n, a, b: pair_sums(n, a, b, 0), normed1, *d_raws)
        m0.exchange("z2")
        h = line.do(back_in, *d_raws, qkv_full)
        h = line.do(core_swap, h)
        m1.halve("z1")
        token_grad, sums1 = line.do(
            lambda p, a, m, g: rows_call(
                kernel(leave_kernel), scalars, [cube(p), a, m], [g],
                [jax.ShapeDtypeStruct(tokens.shape, BF)], True, "leave"),
            h, tokens, d_middle, g1)
        vectors = line.do(
            lambda *v: vectors_call(core, *v[:4], v[4:], offsets, quarter, small.shape[1], pairs),
            sums1, sums2, *col_sums, up_sum, up_sum2)
        vectors = line.do(core_swap, vectors)
        vec_send, vectors = line.do(lambda v: of_y(v[:2] + v[2:]), vectors)
        o_send, o_keep = line.do(
            lambda a, b, d: out_sums(place_at[1:], a, b, d), *attended, d_branch)
        q = start(q_got, q_keep, [half, half], [True, True])
        q.halve("x")
        o = start(y_swap(o_send), o_keep, [quarter], [False])
        m0.back()
        m1.exchange("z2")
        mlp = line.do(
            lambda *v: feed_out(place_at, *v, 1), act, act2, down, down_w, far_mlp[1], far_mlp2[1])
        q.halve("z1")
        o.halve("x")
        m0.join()
        mlp = line.do(core_swap, mlp)
        mixed = line.do(
            lambda p, m, d, token: rows_call(
                kernel(mixed_kernel), jnp.concatenate([y[None], token]).astype(jnp.int32),
                [cube(p), m], [d], [jax.ShapeDtypeStruct(tokens.shape, BF)], False, "mixed")[0],
            mlp, middle, db, line.token)
        line.token = mixed

        def add32(a, b):
            return a + b

        m1.back()
        q.exchange("z2")
        o.halve("z1")
        m0.land()
        vec_got = y_swap(vec_send)
        m1.join()
        vectors = line.do(add32, vectors, vec_got)
        vec_got = swaps["x"](vectors)
        q.back()
        o.exchange("z2")
        vectors = line.do(add32, vectors, vec_got)
        vec_got = swaps["z1"](vectors)
        q.join()
        m1.land()
        o.back()
        vectors = line.do(add32, vectors, vec_got)
        vec_got = swaps["z2"](vectors)
        o.join()
        d0, d0b, u0, u0b = m0.ends()
        d1, d1b, u1, u1b = m1.ends()
        gd = line.do(lambda *v: up32(jnp.concatenate(v, 0)), d0, d0b, d1, d1b)
        where = [(2 * side + core) * ffq + k * fp
                 for k in range(parts) for core in (c, 1 - c) for side in (0, 1)]
        moves = [(2 * k + core, side * fp, fp, 4 * k + 2 * core + side)
                 for k in range(parts) for core in (0, 1) for side in (0, 1)]
        gu = line.do(lambda *v: place(where, v, ff, moves), u0, u0b, u1, u1b)
        vectors = line.do(add32, vectors, vec_got)
        for swap in swaps["rest"]:
            vectors = vectors + swap(vectors)

        where = qkv_starts(c) + qkv_starts(1 - c)
        moves = [(2 * side + core, g * PAIR, PAIR, 6 * pairs * core + 3 * pairs * side + g)
                 for core in (0, 1) for side in (0, 1) for g in range(3 * pairs)]
        gq = line.do(lambda *v: place(where, v, 3 * width, moves), *q.ends())
        o, o2 = o.ends()
        go = line.do(lambda a, b: up32(jnp.concatenate([a, b], 0)), o, o2)
        vectors = line.tie(vectors[0])
        mixed = line.token

        cuts = [vectors[offsets[i]:offsets[i] + quarter] for i in range(6)]
        v_g1, v_b1, v_ob, v_g2, v_b2, v_db = cuts
        v_qv = vectors[offsets[6]:offsets[7]]
        v_ub = vectors[offsets[7]:]
        return (
            mixed, token_grad, v_g1, v_b1, gq, v_qv, go, v_ob, v_g2, v_b2, gu, v_ub, gd, v_db,
        )

    return per_device


def solution(mesh):
    rows = P(("rep", "shard"), None, None)
    vec, mat = P("shard"), P("shard", None)
    return jax.shard_map(
        build(mesh),
        mesh=mesh,
        in_specs=(rows, rows, P(("rep", "shard")), vec, vec, mat, vec, mat, vec, vec, vec,
                  mat, vec, mat, vec),
        out_specs=(rows, rows, vec, vec, mat, vec, mat, vec, vec, vec, mat, vec, mat, vec),
        check_vma=False,
    )
```

```python
import functools
import math

import jax
import jax.numpy as jnp
from jax import lax
from jax.experimental import pallas as pl
from jax.experimental.pallas import tpu as pltpu
from jax.sharding import PartitionSpec as P

HEAD_DIM = 64
PAIR = 2 * HEAD_DIM
EPSILON = 1e-06
BF = jnp.bfloat16
F32 = jnp.float32
NT = ((1,), (1,))
TN = ((0,), (0,))
VMEM_BYTES = 32 << 20


def up32(values):
    return values.astype(F32)


def flip(axis, size, bit):
    pairs = [(i, i ^ bit) for i in range(size)]
    return lambda values: lax.ppermute(values, axis, pairs)


def pick(first, second, index):
    return jnp.where(index == 0, first, second)


def dot(left, right, contract=((1,), (0,))):
    return lax.dot_general(left, right, (contract, ((), ())), preferred_element_type=F32)


def tie(*values):
    return lax.optimization_barrier(values)


def normalize(values):
    average = jnp.mean(values, -1, keepdims=True)
    centered = values - average
    inverse = lax.rsqrt(jnp.mean(centered * centered, -1, keepdims=True) + EPSILON)
    return centered * inverse, inverse


def norm_back(upstream, normed, inverse, gain):
    scaled = upstream * gain
    return inverse * (
        scaled
        - jnp.mean(scaled, -1, keepdims=True)
        - normed * jnp.mean(scaled * normed, -1, keepdims=True)
    )


def gelu_parts(values):
    phi = 0.5 * (1.0 + lax.erf(values * (1.0 / math.sqrt(2.0))))
    slope = phi + values * jnp.exp(-0.5 * values * values) * (1.0 / math.sqrt(2.0 * math.pi))
    return values * phi, slope


def attend_kernel(seq, tile, raw_ref, out_ref, log_ref):
    n = raw_ref.shape[0]
    lane = lax.broadcasted_iota(jnp.int32, (n, PAIR), 1)
    row = lax.broadcasted_iota(jnp.int32, (n, PAIR), 0)
    keys, values = raw_ref[:, PAIR:2 * PAIR], raw_ref[:, 2 * PAIR:]
    one, zero = jnp.asarray(1, BF), jnp.asarray(0, BF)
    low = jnp.asarray(-1e30, BF)
    mine = [(lane // HEAD_DIM) == h for h in (0, 1)]
    spare = [lane == (1 - h) * HEAD_DIM for h in (0, 1)]
    k_of = [jnp.where(mine[h], keys, jnp.where(spare[h] & (row >= seq), low, zero)) for h in (0, 1)]
    v_of = [jnp.where(mine[h], values, one) for h in (0, 1)]
    jobs = [(t, min(tile, n - t), h) for t in range(0, n, tile) for h in (0, 1)]

    def score(job):
        t, m, h = job
        q = raw_ref[t:t + m, :PAIR] * jnp.asarray(1.0 / math.sqrt(HEAD_DIM), BF)
        q = jnp.where(mine[h][t:t + m], q, jnp.where(spare[h][t:t + m], one, zero))
        return dot(q, k_of[h], NT)

    ahead = 2
    ready = [score(job) for job in jobs[:ahead]]
    for i, (t, m, h) in enumerate(jobs):
        if i + ahead < len(jobs):
            ready.append(score(jobs[i + ahead]))
        s = ready.pop(0)
        top = jnp.max(s, -1, keepdims=True)
        res = dot(jnp.exp(s - top).astype(BF), v_of[h])
        own = slice(h * HEAD_DIM, (h + 1) * HEAD_DIM)
        other = slice((1 - h) * HEAD_DIM, (2 - h) * HEAD_DIM)
        total = res[:, other]
        out_ref[t:t + m, own] = (res[:, own] / total).astype(BF)
        log_ref[t:t + m, own] = top + jnp.log(total)


def attend(raw, seq, images, padded, first, groups):
    spec = pl.BlockSpec((padded, PAIR), lambda i, g: (i, g))
    return pl.pallas_call(
        functools.partial(attend_kernel, seq, 304),
        grid=(images, groups),
        in_specs=[pl.BlockSpec((padded, 3 * PAIR), lambda i, g: (i, first + g))],
        out_specs=[spec, spec],
        out_shape=[
            jax.ShapeDtypeStruct((images * padded, groups * PAIR), BF),
            jax.ShapeDtypeStruct((images * padded, groups * PAIR), F32),
        ],
        compiler_params=pltpu.CompilerParams(vmem_limit_bytes=VMEM_BYTES),
        name="attend",
    )(raw)


def attend_back_kernel(seq, wide, raw_ref, d_ref, log_ref, out_ref, sum_ref, kk_ref, vv_ref, p_ref,
                       s_ref):
    n = raw_ref.shape[0]
    scale = 1.0 / math.sqrt(HEAD_DIM)
    lane = lax.broadcasted_iota(jnp.int32, (n, PAIR), 1)
    zero = jnp.asarray(0, BF)
    gap = jnp.zeros((wide - n, PAIR), BF)

    def stacked(v):
        first = lane < HEAD_DIM
        return jnp.concatenate([jnp.where(first, v, zero), gap, jnp.where(first, zero, v), gap], 0)

    kk_ref[:, :PAIR] = stacked(raw_ref[:, PAIR:2 * PAIR])
    vv_ref[...] = stacked(raw_ref[:, 2 * PAIR:])

    @pl.when((pl.program_id(0) == 0) & (pl.program_id(1) == 0))
    def _():
        lanes = lax.broadcasted_iota(jnp.int32, (2 * wide, PAIR), 1)
        row = lax.broadcasted_iota(jnp.int32, (2 * wide, PAIR), 0)
        row = jnp.where(row >= wide, row - wide, row)
        kk_ref[:, PAIR:] = jnp.where((lanes == 0) & (row >= seq), jnp.asarray(-1e30, BF), zero)

    q = raw_ref[:, :PAIR]
    d = d_ref[...]
    mask = jnp.where(lane == 0, jnp.asarray(1, BF), zero)
    s = dot(jnp.concatenate([q * jnp.asarray(scale, BF), mask], 1), kk_ref[...], NT)
    dp = dot(d, vv_ref[...], NT)
    for h in (0, 1):
        cols = slice(h * wide, (h + 1) * wide)
        p = jnp.exp(s[:, cols] - log_ref[:, h * HEAD_DIM:h * HEAD_DIM + 1])
        dph = dp[:, cols]
        p_ref[:, cols] = p.astype(BF)
        s_ref[:, cols] = (p * (dph - jnp.sum(dph * p, -1, keepdims=True))).astype(BF)
    dk = dot(s_ref[...], q, TN)
    dv = dot(p_ref[...], d, TN)
    first = lane < HEAD_DIM
    for j, value in enumerate((
            dot(s_ref[...], kk_ref[:, :PAIR]) * scale,
            jnp.where(first, dk[:n], dk[wide:wide + n]) * scale,
            jnp.where(first, dv[:n], dv[wide:wide + n]))):
        cols = slice(j * PAIR, (j + 1) * PAIR)
        low = value.astype(BF)
        out_ref[:, cols] = low
        sum_ref[0, :, cols] = jnp.broadcast_to(
            jnp.sum(up32(low), 0, keepdims=True), (sum_ref.shape[1], PAIR))


def attend_back(raw, d_att, logs, seq, images, padded, start, groups):
    wide = -(-padded // 128) * 128
    one = pl.BlockSpec((padded, PAIR), lambda i, g: (i, start + g))
    log = pl.BlockSpec((padded, PAIR), lambda i, g: (i, g))
    three = pl.BlockSpec((padded, 3 * PAIR), lambda i, g: (i, start + g))
    cols = groups * 3 * PAIR
    return pl.pallas_call(
        functools.partial(attend_back_kernel, seq, wide),
        grid=(images, groups),
        in_specs=[three, one, log],
        out_specs=[pl.BlockSpec((padded, 3 * PAIR), lambda i, g: (i, g)),
                   pl.BlockSpec((1, 8, 3 * PAIR), lambda i, g: (i, 0, g))],
        out_shape=[jax.ShapeDtypeStruct((raw.shape[0], cols), BF),
                   jax.ShapeDtypeStruct((images, 8, cols), F32)],
        scratch_shapes=[
            pltpu.VMEM((2 * wide, 2 * PAIR), BF),
            pltpu.VMEM((2 * wide, PAIR), BF),
            pltpu.VMEM((padded, 2 * wide), BF),
            pltpu.VMEM((padded, 2 * wide), BF),
        ],
        compiler_params=pltpu.CompilerParams(vmem_limit_bytes=VMEM_BYTES),
        name="attend_back",
    )(raw, d_att, logs)


TILE = 304
WIDE = 512


def whole(array):
    return pl.BlockSpec(array.shape, lambda *_: (0,) * array.ndim)


def params():
    return pltpu.CompilerParams(vmem_limit_bytes=VMEM_BYTES)


def spread_kernel(size, starts, c_ref, w_ref, own_ref, other_ref):
    rows = w_ref.shape[0]
    wide = own_ref.shape[1] // size
    for core in (0, 1):
        @pl.when(c_ref[0] == core)
        def _(core=core):
            for out_ref, columns in ((own_ref, starts[core]), (other_ref, starts[1 - core])):
                for i, start in enumerate(columns):
                    row, col = i // wide * rows, i % wide * size
                    out_ref[row:row + rows, col:col + size] = w_ref[:, start:start + size]


def spread(core, w, starts, size, blocks):
    count = len(starts[0])
    out = jax.ShapeDtypeStruct((w.shape[0] * blocks, count // blocks * size), w.dtype)
    return pl.pallas_call(
        functools.partial(spread_kernel, size, starts),
        grid_spec=pltpu.PrefetchScalarGridSpec(
            num_scalar_prefetch=1, grid=(1,), in_specs=[whole(w)], out_specs=[whole(out)] * 2),
        out_shape=[out] * 2, compiler_params=params(), name="spread")(core, w)


def row_mask(tile, seq):
    return lax.broadcasted_iota(jnp.int32, (TILE, 1), 0) + tile * TILE < seq


def near_first(value, y):
    half = value.shape[1] // 2
    a, b = value[:, :half], value[:, half:]
    return jnp.concatenate([jnp.where(y == 0, a, b), jnp.where(y == 0, b, a)], 1)


def column_sum(value):
    return jnp.sum(value, 0, keepdims=True)


def rows_call(kernel, scalars, arrays, vectors, outs, sums, name):
    images = arrays[-1].shape[-3]
    padded = max(v.shape[-2] for v in (*arrays, *outs))

    def spec(v):
        if len(v.shape) == 3:
            return pl.BlockSpec((1, TILE, v.shape[-1]), lambda i, t, s: (i, t, 0))
        return pl.BlockSpec((2, 1, TILE, v.shape[-1]), lambda i, t, s: (0, i, t, 0))

    width = arrays[0].shape[-1]
    more = [jax.ShapeDtypeStruct((8, width), F32)] if sums else []
    return pl.pallas_call(
        kernel,
        grid_spec=pltpu.PrefetchScalarGridSpec(
            num_scalar_prefetch=1, grid=(images, -(-padded // TILE)),
            in_specs=[*map(spec, arrays), *map(whole, vectors)],
            out_specs=[*map(spec, outs), *map(whole, more)]),
        out_shape=[*outs, *more],
        compiler_params=params(),
        name=name,
    )(scalars, *arrays, *vectors)


def enter_kernel(seq, s_ref, own_ref, other_ref, grad_ref, grad2_ref, gain_ref, shift_ref,
                 norm_ref, out_ref):
    k = pl.program_id(0)
    ok = row_mask(pl.program_id(2), seq)
    mine = k == s_ref[1]
    unit, _ = normalize(up32(jnp.where(mine, own_ref[0], other_ref[0])))
    normed = jnp.where(ok, near_first(unit * gain_ref[...] + shift_ref[...], s_ref[0]), 0.0)
    norm_ref[0, 0] = normed.astype(BF)
    valid = s_ref[2 + k * pl.num_programs(1) + pl.program_id(1)]
    grad = up32(jnp.where(mine, grad_ref[0], grad2_ref[0]))
    out_ref[0, 0] = jnp.where(ok & (valid != 0), grad * up32(valid), 0.0).astype(BF)


def enter(scalars, own, other, grad, grad2, gain, shift, padded):
    images, seq, width = own.shape
    spec = pl.BlockSpec((1, TILE, width), lambda k, i, t, s: (i, t, 0))
    out = jax.ShapeDtypeStruct((2, images, padded, width), BF)
    out_spec = pl.BlockSpec((1, 1, TILE, width), lambda k, i, t, s: (k, i, t, 0))
    return pl.pallas_call(
        functools.partial(enter_kernel, seq),
        grid_spec=pltpu.PrefetchScalarGridSpec(
            num_scalar_prefetch=1, grid=(2, images, -(-padded // TILE)),
            in_specs=[spec] * 4 + [whole(gain), whole(shift)], out_specs=[out_spec] * 2),
        out_shape=[out, out],
        compiler_params=params(),
        name="enter",
    )(scalars, own, other, grad, grad2, gain, shift)


def middle_kernel(seq, s_ref, x_ref, parts_ref, add_ref, gain_ref, shift_ref, mid_ref, norm_ref):
    ok = row_mask(pl.program_id(1), seq)
    middle = up32(x_ref[0]) + (up32(parts_ref[0, 0]) + up32(parts_ref[1, 0])) + add_ref[...]
    middle = jnp.where(ok, middle, 0.0)
    mid_ref[0] = middle
    unit, _ = normalize(middle)
    normed = jnp.where(ok, near_first(unit * gain_ref[...] + shift_ref[...], s_ref[0]), 0.0)
    for k in (0, 1):
        norm_ref[k, 0] = normed.astype(BF)


def start_sums(sum_ref):
    @pl.when((pl.program_id(0) == 0) & (pl.program_id(1) == 0))
    def _():
        sum_ref[...] = jnp.zeros_like(sum_ref)


def back_middle_kernel(seq, s_ref, parts_ref, mid_ref, grad_ref, gain_ref, d_ref, low_ref, sum_ref):
    i = pl.program_id(0)
    ok = row_mask(pl.program_id(1), seq)
    unit, inverse = normalize(mid_ref[0])
    h = near_first(up32(parts_ref[0, 0]) + up32(parts_ref[1, 0]), s_ref[0])
    h = jnp.where(ok, h, 0.0)
    unit = jnp.where(ok, unit, 0.0)
    valid = s_ref[1 + i]
    dy = jnp.where(ok & (valid != 0), up32(grad_ref[0]) * up32(valid), 0.0)
    d_middle = jnp.where(ok, dy + norm_back(h, unit, inverse, gain_ref[...]), 0.0)
    low = d_middle.astype(BF)
    d_ref[0] = d_middle
    for k in (0, 1):
        low_ref[k, 0] = low
    start_sums(sum_ref)
    for row, value in enumerate((h * unit, h, up32(low), up32(dy.astype(BF)))):
        sum_ref[row:row + 1, :] += column_sum(value)


def leave_kernel(seq, s_ref, parts_ref, x_ref, mid_ref, gain_ref, d_ref, sum_ref):
    ok = row_mask(pl.program_id(1), seq)
    unit, inverse = normalize(up32(x_ref[0]))
    h = near_first(up32(parts_ref[0, 0]) + up32(parts_ref[1, 0]), s_ref[0])
    h = jnp.where(ok, h, 0.0)
    d_ref[0] = (mid_ref[0] + norm_back(h, unit, inverse, gain_ref[...])).astype(BF)
    start_sums(sum_ref)
    for row, value in enumerate((jnp.where(ok, h * unit, 0.0), h)):
        sum_ref[row:row + 1, :] += column_sum(value)


def place_kernel(count, moves, where_ref, *refs):
    ins, out_ref = refs[:count], refs[count]
    x = where_ref[0]
    for numbers, row, col, size, entry in moves:
        rows = slice(row, row + out_ref.shape[0])
        a, b = [up32(ins[i][rows, col:col + size]) for i in (numbers * 2)[:2]]
        start = pl.multiple_of(where_ref[1 + entry], 128)
        out_ref[:, pl.ds(start, size)] = jnp.where(x == 0, a, b)


def place(x, where, inputs, rows, width, moves):
    out = jax.ShapeDtypeStruct((rows, width), F32)
    return pl.pallas_call(
        functools.partial(place_kernel, len(inputs), moves),
        grid_spec=pltpu.PrefetchScalarGridSpec(
            num_scalar_prefetch=1, grid=(1,), in_specs=[whole(v) for v in inputs],
            out_specs=whole(out)),
        out_shape=out,
        compiler_params=params(),
        name="place",
    )(jnp.stack([jnp.asarray(w, jnp.int32) for w in [x, *where]]), *inputs)


def halves_kernel(s_ref, *refs):
    out_ref = refs[-1]
    h = pl.program_id(0) % 2
    for k in range(len(refs) // 2):
        @pl.when(pl.program_id(0) // 2 == k)
        def _(keep_ref=refs[2 * k], got_ref=refs[2 * k + 1]):
            out_ref[...] = up32(jnp.where(s_ref[0] == h, keep_ref[...], got_ref[...]))


def halves(x, pairs, rows):
    width = pairs[0].shape[1]
    spec = pl.BlockSpec((rows, width), lambda i, s: (0, 0))
    return pl.pallas_call(
        halves_kernel,
        grid_spec=pltpu.PrefetchScalarGridSpec(
            num_scalar_prefetch=1, grid=(len(pairs),), in_specs=[spec] * len(pairs),
            out_specs=pl.BlockSpec((rows, width), lambda i, s: (i, 0))),
        out_shape=jax.ShapeDtypeStruct((len(pairs) * rows, width), F32),
        compiler_params=params(),
        name="halves",
    )(x, *pairs)


def pack_kernel(*refs):
    at = 0
    for ref in refs[:-1]:
        refs[-1][:, at:at + ref.shape[1]] = up32(ref[...])
        at += ref.shape[1]


def pack(*vectors):
    vectors = [v[None] for v in vectors]
    out = jax.ShapeDtypeStruct((1, sum(v.shape[1] for v in vectors)), F32)
    return pl.pallas_call(
        pack_kernel, grid=(1,), in_specs=[whole(v) for v in vectors], out_specs=whole(out),
        out_shape=out, compiler_params=params(), name="pack")(*vectors)


def small_kernel(offsets, quarter, parts, pairs, c_ref, all_ref, vec_ref, bias_ref, upb_ref):
    c = c_ref[0]

    def of(shard, start, size):
        row = shard % 2 * 2 + shard // 2
        return all_ref[row:row + 1, start:start + size]

    for row, at in enumerate(offsets[:6]):
        for q in range(4):
            vec_ref[row:row + 1, q * quarter:(q + 1) * quarter] = of(q, at, quarter)
    qv, up = offsets[6:]

    def block(b):
        return of(b // 2, qv + b % 2 * quarter, quarter)

    for side in (0, 1):
        for part in range(3):
            if part == 1:
                value = jnp.zeros((1, quarter), F32)
            else:
                b = 2 * part + 2 * side
                value = jnp.where(c == 0, block(b), block(b + 1))
            for g in range(pairs):
                to = ((side * pairs + g) * 3 + part) * PAIR
                bias_ref[:, to:to + PAIR] = value[:, g * PAIR:(g + 1) * PAIR]
    fp = upb_ref.shape[1] // 2 // parts
    for k in range(parts):
        for side in (0, 1):
            to = (2 * k + side) * fp
            start = up + k * fp
            upb_ref[:, to:to + fp] = jnp.where(
                c == 0, of(2 * side, start, fp), of(2 * side + 1, start, fp))


def small_call(core, gathered, offsets, quarter, ffq, parts, pairs):
    shapes = [jax.ShapeDtypeStruct(s, F32)
              for s in ((8, 4 * quarter), (1, 6 * quarter), (1, 2 * ffq))]
    return pl.pallas_call(
        functools.partial(small_kernel, offsets, quarter, parts, pairs),
        grid_spec=pltpu.PrefetchScalarGridSpec(
            num_scalar_prefetch=1, grid=(1,), in_specs=[whole(gathered)],
            out_specs=[whole(s) for s in shapes]),
        out_shape=shapes,
        compiler_params=params(),
        name="small",
    )(core, gathered)


def vectors_kernel(offsets, quarter, parts, pairs, c_ref, one_ref, two_ref, low_ref, high_ref, *refs):
    ups, out_ref = refs[:parts], refs[parts]
    c = c_ref[0]
    rows = ((one_ref, 0), (one_ref, 1), (two_ref, 2), (two_ref, 0), (two_ref, 1), (two_ref, 3))
    qv, up = offsets[6:]

    def sums(ref, part):
        total = jnp.sum(ref[:, 0, :], 0, keepdims=True)
        return jnp.concatenate(
            [total[:, (3 * g + part) * PAIR:(3 * g + part + 1) * PAIR] for g in range(pairs)], 1)

    table = [[sums(ref, part) for part in (0, 2)] for ref in (low_ref, high_ref)]
    fp = ups[0].shape[1] // 2
    for core in (0, 1):
        for side in (0, 1):
            to = 2 * core + side
            shard = 2 * side + core
            for (ref, row), at in zip(rows, offsets[:6]):
                out_ref[to:to + 1, at:at + quarter] = (
                    ref[row:row + 1, shard * quarter:(shard + 1) * quarter])
            for h in (0, 1):
                block = 2 * shard + h
                value = table[block % 4 // 2][block // 4]
                out_ref[to:to + 1, qv + h * quarter:qv + (h + 1) * quarter] = jnp.where(
                    c == block % 2, value, 0.0)
            for k, ref in enumerate(ups):
                out_ref[to:to + 1, up + k * fp:up + (k + 1) * fp] = jnp.where(
                    c == core, ref[:, side * fp:(side + 1) * fp], 0.0)


def vectors_call(core, one, two, low, high, ups, offsets, quarter, width, pairs):
    out = jax.ShapeDtypeStruct((4, width), F32)
    ins = [one, two, low, high, *ups]
    return pl.pallas_call(
        functools.partial(vectors_kernel, offsets, quarter, len(ups), pairs),
        grid_spec=pltpu.PrefetchScalarGridSpec(
            num_scalar_prefetch=1, grid=(1,), in_specs=[whole(v) for v in ins],
            out_specs=whole(out)),
        out_shape=out,
        compiler_params=params(),
        name="vectors",
    )(core, *ins)


def feed_kernel(s_ref, n2_ref, do_ref, own_ref, other_ref, ua_ref, ub_ref, near_ref, da_ref,
                db_ref, bias_ref, h_ref, act_ref, keep_ref, send_ref, hsum_ref,
                sum_ref, up_ref, down_ref, acc_ref):
    x, y = s_ref[0], s_ref[1]
    j = pl.program_id(0)
    steps = pl.num_programs(0)
    half = steps // 2
    wide = up_ref.shape[1]
    quarter = own_ref.shape[0]
    up_ref[:quarter, :] = own_ref[...]
    up_ref[quarter:2 * quarter, :] = other_ref[...]
    a, b = ua_ref[...], ub_ref[...]
    up_ref[2 * quarter:3 * quarter, :] = jnp.where(x == 0, a, b)
    up_ref[3 * quarter:, :] = jnp.where(x == 0, b, a)
    near = j // half == y

    @pl.when(near)
    def _():
        down_ref[...] = near_ref[...]

    @pl.when(jnp.logical_not(near))
    def _():
        down_ref[...] = jnp.where((x == 0) == (j % half == 0), da_ref[...], db_ref[...])

    n2, do = n2_ref[...], do_ref[...]
    act, slope = gelu_parts(dot(n2, up_ref[...]) + bias_ref[...])
    act = act.astype(BF)
    act_ref[...] = act
    d_pre = (dot(do, down_ref[...], NT) * slope).astype(BF)
    sum_ref[...] = jnp.sum(up32(d_pre), 0, keepdims=True)
    gd = dot(act, do, TN).astype(BF)
    at_rows = pl.ds(pl.multiple_of(j % half * wide, wide), wide)

    @pl.when(near)
    def _():
        keep_ref[at_rows, :] = gd

    @pl.when(jnp.logical_not(near))
    def _():
        send_ref[at_rows, :] = gd

    gu = dot(n2, d_pre, TN).astype(BF)
    cols = pl.ds(pl.multiple_of(j * wide, wide), wide)
    keep_ref[half * wide:, cols] = gu[:2 * quarter]
    send_ref[half * wide:, cols] = gu[2 * quarter:]

    @pl.when(j == 0)
    def _():
        acc_ref[...] = h_ref[...]

    acc_ref[...] += dot(d_pre, up_ref[...], NT)

    @pl.when(j == steps - 1)
    def _():
        hsum_ref[...] = acc_ref[...].astype(BF)


def feed(scalars, n2, do, near_up, a, b, down, bias, h, k, wide=256):
    both, width = n2.shape
    quarter = width // 4
    cols = bias.shape[1]
    half = cols // 2 // wide
    parts = near_up.shape[0] // 2 // quarter
    n2_spec = whole(n2)
    piece = jax.ShapeDtypeStruct((cols // 2 + width // 2, width), BF)
    low = jax.ShapeDtypeStruct((both, width), BF)

    def near(j, s):
        return (k * half + jnp.where(j // half == s[1], j % half, 0), 0)

    return pl.pallas_call(
        feed_kernel,
        grid_spec=pltpu.PrefetchScalarGridSpec(
            num_scalar_prefetch=1, grid=(2 * half,),
            in_specs=[
                n2_spec, n2_spec,
                pl.BlockSpec((quarter, wide), lambda j, s: (k, j)),
                pl.BlockSpec((quarter, wide), lambda j, s: (parts + k, j)),
                pl.BlockSpec((quarter, wide), lambda j, s: (0, j)),
                pl.BlockSpec((quarter, wide), lambda j, s: (0, j)),
                pl.BlockSpec((wide, width), near),
                pl.BlockSpec((wide, width), lambda j, s: (quarter // wide, 0)),
                pl.BlockSpec((wide, width), lambda j, s: (quarter // wide, 0)),
                pl.BlockSpec((1, wide), lambda j, s: (0, j)),
                whole(h)],
            out_specs=[
                pl.BlockSpec((both, wide), lambda j, s: (0, j)),
                whole(piece), whole(piece),
                whole(low),
                pl.BlockSpec((1, wide), lambda j, s: (0, j))],
            scratch_shapes=[pltpu.VMEM((width, wide), BF), pltpu.VMEM((wide, width), BF),
                            pltpu.VMEM((both, width), F32)]),
        out_shape=[jax.ShapeDtypeStruct((both, cols), BF), piece, piece, low,
                   jax.ShapeDtypeStruct((1, cols), F32)],
        compiler_params=pltpu.CompilerParams(vmem_limit_bytes=58 << 20),
        name="feed",
    )(scalars, n2, do, near_up, near_up, a, b, down, a, b, bias, h)


def halve_kernel(sizes, s_ref, keep_ref, got_ref, mine_ref, theirs_ref):
    at = 0
    for i, size in enumerate(sizes):
        n = size // 2
        for bit, out_ref in ((s_ref[i], mine_ref), (1 - s_ref[i], theirs_ref)):
            rows = pl.ds(pl.multiple_of(at + bit * n, 16), n)
            out_ref[at // 2:at // 2 + n, :] = added(keep_ref[rows, :], got_ref[rows, :])
        at += size


def add_kernel(keep_ref, got_ref, out_ref):
    out_ref[...] = added(keep_ref[...], got_ref[...])


def other_kernel(sizes, cross, s_ref, keep_ref, got_ref, out_ref):
    at, to = 0, 0
    for size, crosses in zip(sizes, cross):
        if crosses:
            out_ref[to:to + size, :] = jnp.where(
                s_ref[0] == 0, got_ref[at:at + size, :], keep_ref[at:at + size, :])
            to += size
        at += size


def join_kernel(sizes, s_ref, keep_ref, got_ref, out_ref):
    at = 0
    for size in sizes:
        rows = slice(at, at + size)
        keep, got = keep_ref[rows, :], got_ref[rows, :]
        out_ref[2 * at:2 * at + size, :] = jnp.where(s_ref[0] == 0, keep, got)
        out_ref[2 * at + size:2 * (at + size), :] = jnp.where(s_ref[0] == 0, got, keep)
        at += size


def columns_call(kernel, scalars, arrays, rows, block, outs, name):
    cols = arrays[0].shape[1]
    width = WIDE if cols % WIDE == 0 else cols // 2
    spec = pl.BlockSpec((rows, width), lambda j, *_: (block, j))
    out_specs = [pl.BlockSpec((n, width), lambda j, *_: (0, j)) for n in outs]
    return pl.pallas_call(
        kernel,
        grid_spec=pltpu.PrefetchScalarGridSpec(
            num_scalar_prefetch=len(scalars), grid=(cols // width,),
            in_specs=[spec] * len(arrays), out_specs=out_specs),
        out_shape=[jax.ShapeDtypeStruct((n, cols), BF) for n in outs],
        compiler_params=params(),
        name=name,
    )(*scalars, *arrays)


def pair_kernel(n_ref, a_ref, b_ref, out_ref):
    for j, ref in enumerate((a_ref, b_ref)):
        @pl.when(pl.program_id(0) == j)
        def _(ref=ref):
            out_ref[...] = dot(n_ref[...], ref[...], TN).astype(BF)


def pair_sums(n, a, b, side):
    rows, half = n.shape[0], n.shape[1] // 2
    cols = a.shape[1]
    return pl.pallas_call(
        pair_kernel,
        grid=(2,),
        in_specs=[pl.BlockSpec((rows, half), lambda j: (0, side)), whole(a), whole(b)],
        out_specs=pl.BlockSpec((half, cols), lambda j: (j, 0)),
        out_shape=jax.ShapeDtypeStruct((2 * half, cols), BF),
        compiler_params=params(),
        name="pair_sums",
    )(n, a, b)


def back_in_kernel(a_ref, b_ref, w_ref, out_ref):
    cut = a_ref.shape[1]
    total = dot(a_ref[...], w_ref[:, :cut], NT) + dot(b_ref[...], w_ref[:, cut:], NT)
    out_ref[...] = total.astype(BF)


def back_in(a, b, w, wide=512):
    out = jax.ShapeDtypeStruct((a.shape[0], w.shape[0]), BF)
    return pl.pallas_call(
        back_in_kernel,
        grid=(w.shape[0] // wide,),
        in_specs=[whole(a), whole(b), pl.BlockSpec((wide, w.shape[1]), lambda j: (j, 0))],
        out_specs=pl.BlockSpec((a.shape[0], wide), lambda j: (0, j)),
        out_shape=out,
        compiler_params=params(),
        name="back_in",
    )(a, b, w)


def out_sums_kernel(s_ref, a_ref, b_ref, d_ref, send_ref, keep_ref):
    d = d_ref[...]
    for j, out_ref in enumerate((send_ref, keep_ref)):
        for y, ref in enumerate((a_ref, b_ref)):
            @pl.when((pl.program_id(0) == j) & (s_ref[0] == (y ^ 1 ^ j)))
            def _(ref=ref, out_ref=out_ref):
                out_ref[...] = dot(ref[...], d, TN).astype(BF)


def out_sums(scalars, a, b, d):
    out = jax.ShapeDtypeStruct((a.shape[1], d.shape[1]), BF)
    return pl.pallas_call(
        out_sums_kernel,
        grid_spec=pltpu.PrefetchScalarGridSpec(
            num_scalar_prefetch=1, grid=(2,), in_specs=[whole(a), whole(b), whole(d)],
            out_specs=[whole(out)] * 2),
        out_shape=[out] * 2,
        compiler_params=params(),
        name="out_sums",
    )(scalars, a, b, d)


def feed_out_kernel(s_ref, one_ref, two_ref, down_ref, near_ref, a_ref, b_ref, out_ref):
    x, y = s_ref[0], s_ref[1]
    n = near_ref.shape[0]
    total = dot(one_ref[...], down_ref[...])
    total += dot(two_ref[:, pl.ds(pl.multiple_of(y * n, n), n)], near_ref[...])
    a, b = a_ref[...], b_ref[...]
    for i, w in enumerate((jnp.where(x == 0, a, b), jnp.where(x == 0, b, a))):
        start = pl.multiple_of((1 - y) * n + i * (n // 2), n // 2)
        total += dot(two_ref[:, pl.ds(start, n // 2)], w)
    out_ref[...] = total.astype(BF)


def feed_out(scalars, one, two, down, near, a, b, k, wide=512):
    rows, cols = one.shape[0], down.shape[1]
    n = two.shape[1] // 2
    return pl.pallas_call(
        feed_out_kernel,
        grid_spec=pltpu.PrefetchScalarGridSpec(
            num_scalar_prefetch=1, grid=(cols // wide,),
            in_specs=[
                whole(one), whole(two), pl.BlockSpec((down.shape[0], wide), lambda j, s: (0, j)),
                pl.BlockSpec((n, wide), lambda j, s: (k, j)),
                pl.BlockSpec((n // 2, wide), lambda j, s: (1, j)),
                pl.BlockSpec((n // 2, wide), lambda j, s: (1, j))],
            out_specs=pl.BlockSpec((rows, wide), lambda j, s: (0, j))),
        out_shape=jax.ShapeDtypeStruct((rows, cols), BF),
        compiler_params=params(),
        name="feed_out",
    )(scalars, one, two, down, near, a, b)


ORDER = (
    "swap_h", "back_mid", "swap_d", "m0.x", "to_heads", "out_send", "attend_0", "attend_1", "m0.z1",
    "m1.x", "q_send", "q_keep", "to_input", "swap_in", "m0.z2", "leave", "small_sums", "m1.z1",
    "to_mixed", "q.x", "small_y", "m0.back", "m1.z2", "rest", "q.z1", "m0.join", "r.x", "m1.back",
    "q.z2", "r.zz", "m1.join", "m0.over", "q.back", "r.z2", "q.join", "m1.over", "rest_back",
    "q.over", "swap_mixed", "grad_down", "mixed", "grad_up",
)


class Line:
    def __init__(self, token):
        self.token = token

    def tie(self, *values):
        *values, self.token = lax.optimization_barrier((*values, self.token))
        return values[0] if len(values) == 1 else values

    def do(self, step, *values):
        values = self.tie(*values)
        out = step(*values) if isinstance(values, list) else step(values)
        return self.tie(*out) if isinstance(out, (list, tuple)) else self.tie(out)


def added(keep, got):
    return (up32(keep) + up32(got)).astype(BF)


class Sum:
    def __init__(self, line, swaps, at, got, keep, sizes, cross, block=0):
        self.line, self.swaps, self.at, self.cross = line, swaps, at, cross
        self.got, self.keep, self.sizes, self.block = got, keep, sizes, block

    def run(self, kernel, bits, outs, name):
        scalars = [jnp.stack(bits).astype(jnp.int32)] if bits else []
        out = self.line.do(
            lambda keep, got: columns_call(
                kernel, scalars, [keep, got], sum(self.sizes), self.block, outs, name),
            self.keep, self.got)
        self.block = 0
        return out

    def halve(self, axis):
        bits = [self.at["cross" if cross and axis == "x" else axis] for cross in self.cross]
        n = sum(self.sizes) // 2
        self.keep, theirs = self.run(
            functools.partial(halve_kernel, self.sizes), bits, [n, n], "halve")
        self.sizes = [n // 2 for n in self.sizes]
        self.got = self.swaps[axis](theirs)

    def add(self):
        self.keep = self.run(add_kernel, [], [sum(self.sizes)], "add")

    def exchange(self, axis):
        self.add()
        self.got = self.swaps[axis](self.keep)

    def back(self):
        self.add()
        for swap in self.swaps["rest"]:
            self.got = swap(self.keep)
            self.add()
        self.got = self.swaps["z1"](self.keep)

    def join(self):
        self.keep = self.run(
            functools.partial(join_kernel, self.sizes), [self.at["z1"]], [2 * sum(self.sizes)], "join")
        self.sizes = [2 * n for n in self.sizes]
        self.got = self.swaps["x"](self.keep)

    def land(self):
        self.got = self.line.tie(self.got)

    def cross_over(self):
        rows = sum(n for n, cross in zip(self.sizes, self.cross) if cross)
        self.keep, self.got = self.line.tie(self.keep, self.got)
        other = self.run(
            functools.partial(other_kernel, self.sizes, self.cross), [self.at["x"]], [rows], "other")
        self.other = self.swaps["core"](other)


def build(mesh):
    reps = mesh.shape["rep"]
    shards = mesh.shape["shard"]
    y_swap = flip("shard", shards, 2)
    cores = [[2 * i, 2 * i + 1] for i in range(shards // 2)]
    bits = [1 << i for i in range(reps.bit_length() - 1)]
    rep_swap = {b: flip("rep", reps, b) for b in bits}

    def core_swap(values):
        return lax.all_to_all(values, "shard", 0, 0, axis_index_groups=cores, tiled=True)

    swaps = {"core": flip("shard", shards, 1), "y": y_swap, "x": rep_swap[bits[0]], "z1": rep_swap[bits[1]],
             "z2": rep_swap[bits[2]], "rest": [rep_swap[b] for b in bits[3:]]}

    def per_device(
        tokens, out_grad, valid, attn_gain, attn_shift, qkv_w, qv_b, out_w, out_b,
        mlp_gain, mlp_shift, up_w, up_b, down_w, down_b,
    ):
        images, seq, width = tokens.shape
        ff = up_w.shape[1]
        quarter = width // shards
        half = width // 2
        ffq = ff // shards
        padded = -(-seq // 16) * 16
        rows = images * padded
        shard = lax.axis_index("shard")
        rep = lax.axis_index("rep")
        y, c = shard // 2, shard % 2
        x = rep % 2
        at = {"x": x, "z1": (rep // 2) % 2, "z2": (rep // 4) % 2, "cross": x ^ c}
        pairs = quarter // PAIR
        parts = 2
        fp = ffq // parts
        core = c[None].astype(jnp.int32)
        scalars = jnp.concatenate([y[None], valid]).astype(jnp.int32)
        place_at = jnp.stack([x, y]).astype(jnp.int32)

        def qkv_starts(core):
            return [part * width + (2 * side + core) * quarter + g * PAIR
                    for side in (0, 1) for g in range(pairs) for part in range(3)]

        def up_starts(core):
            return [(2 * side + core) * ffq + k * fp for k in range(parts) for side in (0, 1)]

        def by_x(v):
            n = v.shape[0] // 2
            return lax.dynamic_slice_in_dim(v, x * n, n, 0)

        def in_order(got, swapped):
            return [pick(got, swapped, x), pick(swapped, got, x)]

        line = Line(valid)
        core_permute = swaps["core"]

        def for_core(v, which):
            n = v.shape[0] // 2
            return lax.dynamic_slice_in_dim(v, which * n, n, 0)

        def by_core(own, other):
            return [pick(own, other, c), pick(other, own, c)]

        tokens2, grad2 = core_permute(tokens), core_permute(out_grad)
        own_qkv, give = line.do(
            lambda w: spread(core, w, [qkv_starts(0), qkv_starts(1)], PAIR, 1), qkv_w)
        other_qkv = core_permute(give)
        own_up, give = line.do(
            lambda w: spread(core, w, [up_starts(0), up_starts(1)], fp, parts), up_w)
        other_up = core_permute(give)
        far = y_swap(line.do(lambda a, b: pick(a, b, x ^ c), own_qkv, other_qkv))
        small = line.do(pack, attn_gain, attn_shift, out_b, mlp_gain, mlp_shift, down_b, qv_b, up_b,
                        jnp.pad(up32(valid), (0, 128 - images)))
        offsets = [i * quarter for i in range(7)] + [8 * quarter]
        far_small = y_swap(small)
        near_up = line.do(
            lambda a, b: jnp.concatenate(by_core(a, b), 0), own_up, other_up)
        out_w = line.tie(out_w)
        far_out = y_swap(out_w)

        def far_part(k):
            def step(a, w):
                at = (parts * x + k) * quarter
                return jnp.concatenate([
                    lax.dynamic_slice_in_dim(a, at, quarter, 0), by_x(w[k * fp:(k + 1) * fp])], 0)

            return y_swap(line.do(step, near_up, down_w))

        far_mlp, far_mlp2 = [far_part(0)], []
        far = line.tie(far)
        far2 = swaps["x"](far)
        small = line.do(
            lambda a, b: jnp.concatenate([pick(a, b, y), pick(b, a, y)] * 2, 0), small, far_small)
        small = line.do(core_swap, small)
        tokens2, grad2 = line.tie(tokens2, grad2)
        vec, bias, upb = line.do(
            lambda v: small_call(core, v, offsets, quarter, ffq, parts, pairs), small)
        g1, b1, ob, g2, b2, db = [vec[i:i + 1] for i in range(6)]

        def shaped(dtype, *lead):
            return jax.ShapeDtypeStruct((*lead, images, padded, width), dtype)

        def cube(v):
            return v.reshape(2, images, padded, width)

        def flat(v):
            return v.reshape(2 * rows, width)

        def kernel(body):
            return functools.partial(body, seq)

        both = jnp.stack([pick(small[2 * k], small[2 * k + 1], y)[-128:images - 128] for k in (0, 1)])
        normed1, d_out = line.do(
            lambda *v: enter(
                jnp.concatenate([jnp.stack([y, c]), both.reshape(-1).astype(jnp.int32)]).astype(
                    jnp.int32), *v, padded),
            tokens, tokens2, out_grad, grad2, g1, b1)
        normed1, d_out = flat(normed1), flat(d_out)
        far_mlp.append(far_part(1))
        far2 = line.tie(far2)
        qkv_full = line.do(
            lambda a, o, b, d: jnp.concatenate(
                [*by_core(a, o), *in_order(b, d)], 0), own_qkv, other_qkv, far, far2)
        raw = line.do(
            lambda n, w, b: (dot(n, w) + b).astype(BF), normed1, qkv_full, bias)
        far_out = line.tie(far_out)

        def attention(first):
            return line.do(lambda v: attend(v, seq, 2 * images, padded, first, pairs), raw)

        def by_y(near, far):
            return [pick(near, far, y), pick(far, near, y)]

        attended, logs = [None] * 2, [None] * 2
        attended[0], logs[0] = attention(0)
        out_full = line.do(lambda a, b: jnp.concatenate(by_y(a, b), 0), out_w, far_out)
        far_mlp[0] = line.tie(far_mlp[0])
        far_mlp2.append(swaps["x"](far_mlp[0]))
        attended[1], logs[1] = attention(pairs)
        branch = line.do(
            lambda a, b, w: (dot(a, w[:quarter]) + dot(b, w[quarter:])).astype(BF),
            *attended, out_full)
        branch = line.do(core_swap, branch)
        middle, normed2 = line.do(
            lambda a, p, *v: rows_call(
                kernel(middle_kernel), scalars, [a, cube(p)], v, [shaped(F32), shaped(BF, 2)],
                False, "middle"),
            tokens, branch, ob, g2, b2)
        normed2 = line.do(core_swap, flat(normed2))
        far_mlp[1] = line.tie(far_mlp[1])
        far_mlp2.append(swaps["x"](far_mlp[1]))

        def tn(a, b):
            return dot(a, b, TN).astype(BF)

        def of_y(v):
            n = v.shape[0] // 2
            return [lax.dynamic_slice_in_dim(v, side * n, n, 0) for side in (1 - y, y)]

        def start(got, keep, sizes, cross, block=0):
            return Sum(line, swaps, at, got, keep, sizes, cross, block)

        n = fp // 2

        def whole_up(a, b, d):
            return jnp.concatenate(
                [a[:quarter], a[parts * quarter:(parts + 1) * quarter],
                 *in_order(b[:quarter], d[:quarter])], 0)

        def whole_down(k):
            def step(near, a, b):
                near, (a, b) = near[k * fp:(k + 1) * fp], in_order(a[quarter:], b[quarter:])
                return jnp.concatenate(
                    [pick(near[:n], a, y), pick(near[n:], b, y),
                     pick(a, near[:n], y), pick(b, near[n:], y)], 0)

            return line.do(step, down_w, far_mlp[k], far_mlp2[k])

        up = line.do(whole_up, near_up, far_mlp[0], far_mlp2[0])

        def forward(n, w, b):
            act, slope = gelu_parts(dot(n, w) + b)
            return act.astype(BF), slope

        act, slope = line.do(forward, normed2, up, upb[:, :2 * fp])
        d_send, d_keep = line.do(of_y, line.do(tn, act, d_out))
        down = whole_down(0)

        def backward(d, w, sl):
            d_pre = (dot(d, w, NT) * sl).astype(BF)
            return d_pre, jnp.sum(up32(d_pre), 0, keepdims=True)

        d_pre, up_sum = line.do(backward, d_out, down, slope)
        far_mlp2[1] = line.tie(far_mlp2[1])
        m_got = y_swap(line.do(
            lambda n, d, v: jnp.concatenate([v, tn(n[:, half:], d)], 0), normed2, d_pre, d_send))
        m_keep = line.do(
            lambda n, d, v: jnp.concatenate([v, tn(n[:, :half], d)], 0), normed2, d_pre, d_keep)
        m0 = start(m_got, m_keep, [fp, half], [False, True])
        h = line.do(lambda d, w: dot(d, w, NT), d_pre, up)
        act2, keep, send, h, up_sum2 = line.do(
            lambda *v: feed(place_at, *v, 1),
            normed2, d_out, near_up, far_mlp[1], far_mlp2[1], down_w, upb[:, 2 * fp:], h)
        m1 = start(y_swap(send), keep, [fp, half], [False, True])
        have = {"h": h}

        def swap_h():
            have["h"] = line.do(core_swap, have["h"])

        def back_mid():
            have["d_middle"], d_branch, have["sums2"] = line.do(
                lambda p, m, d, g: rows_call(
                    kernel(back_middle_kernel), scalars, [cube(p), m, d], [g],
                    [shaped(F32), shaped(BF, 2)], True, "back_middle"),
                have["h"], middle, out_grad, g2)
            have["d_branch"] = flat(d_branch)

        def swap_d():
            have["d_branch"] = line.do(core_swap, have["d_branch"])

        def to_heads():
            have["d_att"] = line.do(
                lambda d, w: dot(d, w, NT).astype(BF), have["d_branch"], out_full)

        def attention_back(first):
            have["d_raw", first], have["col", first] = line.do(
                lambda a, b, c: attend_back(a, b, c, seq, 2 * images, padded, first, pairs),
                raw, have["d_att"], logs[first // pairs])

        def d_raws():
            return have["d_raw", 0], have["d_raw", pairs]

        def q_send():
            have["q_got"] = y_swap(line.do(
                lambda n, a, b: pair_sums(n, a, b, 1), normed1, *d_raws()))

        def q_keep():
            keep = line.do(lambda n, a, b: pair_sums(n, a, b, 0), normed1, *d_raws())
            have["q"] = start(have["q_got"], keep, [half, half], [True, True])

        def to_input():
            have["h"] = line.do(back_in, *d_raws(), qkv_full)

        def leave():
            token_grad, have["sums1"] = line.do(
                lambda p, a, m, g, token: rows_call(
                    kernel(leave_kernel), jnp.concatenate([y[None], token]).astype(jnp.int32),
                    [cube(p), a, m], [g], [jax.ShapeDtypeStruct(tokens.shape, BF)], True, "leave"),
                have["h"], tokens, have["d_middle"], g1, line.token)
            line.token = token_grad

        def small_sums():
            v = line.do(
                lambda *v: vectors_call(
                    core, *v[:4], v[4:], offsets, quarter, small.shape[1] - 128, pairs),
                have["sums1"], have["sums2"], have["col", 0], have["col", pairs], up_sum, up_sum2)
            sent, have["v"] = line.do(lambda v: (for_core(v, 1 - c), for_core(v, c)), v)
            have["v_got"] = core_permute(sent)

        def small_y():
            sent, have["v"] = line.do(lambda a, b: of_y(a + b), have["v"], have["v_got"])
            have["v_got"] = y_swap(sent)

        def out_send():
            sent, have["o"] = line.do(
                lambda a, b, d: out_sums(place_at[1:], a, b, d), *attended, have["d_branch"])
            have["o_got"] = y_swap(sent)

        def below(top, v):
            v = v.reshape(-1, width).astype(BF)
            return jnp.concatenate([top, jnp.pad(v, ((0, 32 - v.shape[0]), (0, 0)))], 0)

        def rest():
            have["r"] = start(
                line.do(below, have["o_got"], have["v_got"]), line.do(below, have["o"], have["v"]),
                [quarter, 32], [False, False])

        def rest_back():
            r = have["r"]
            r.add()
            for swap in swaps["rest"]:
                r.got = swap(r.keep)
                r.add()
            r.got = swaps["x"](r.keep)

        def to_mixed():
            have["mlp"] = line.do(
                lambda *v: feed_out(place_at, *v, 1),
                act, act2, down, down_w, far_mlp[1], far_mlp2[1])

        def swap_mixed():
            have["mlp_got"] = core_permute(line.do(lambda v: for_core(v, 1 - c), have["mlp"]))

        def mixed():
            have["mixed"] = line.do(
                lambda v, got, m, d: (
                    m + (up32(for_core(v, c)) + up32(got)).reshape(m.shape) + d).astype(BF)[:, :seq],
                have["mlp"], have["mlp_got"], middle, db)

        def grad_down():
            have["down"] = line.do(
                lambda *v: halves(x[None].astype(jnp.int32), v, fp // 2),
                m0.keep, m0.got, m1.keep, m1.got)

        def grad_up():
            where = [(2 * side + core) * ffq + k * fp
                     for k in range(parts) for core in (c, 1 - c) for side in (0, 1)]
            moves = []
            for k in range(parts):
                for side in (0, 1):
                    moves.append(((3 * k, 3 * k + 1), m0.sizes[0], side * fp, fp, 4 * k + side))
                    moves.append(((3 * k + 2,), 0, side * fp, fp, 4 * k + 2 + side))
            have["up"] = line.do(
                lambda *v: place(x, where, v, quarter, ff, moves),
                m0.keep, m0.got, m0.other, m1.keep, m1.got, m1.other)

        plain = {
            "swap_h": swap_h, "swap_in": swap_h, "back_mid": back_mid, "swap_d": swap_d, "to_heads": to_heads,
            "attend_0": lambda: attention_back(0), "attend_1": lambda: attention_back(pairs),
            "q_send": q_send, "q_keep": q_keep, "to_input": to_input, "leave": leave,
            "small_sums": small_sums, "small_y": small_y, "out_send": out_send, "rest": rest,
            "rest_back": rest_back, "to_mixed": to_mixed, "swap_mixed": swap_mixed, "mixed": mixed,
            "grad_down": grad_down, "grad_up": grad_up,
        }
        have.update(m0=m0, m1=m1)
        for name in ORDER:
            if name in plain:
                plain[name]()
                continue
            piece, step = name.split(".")
            piece = have[piece]
            if step in ("back", "join", "over"):
                {"back": piece.back, "join": piece.join, "over": piece.cross_over}[step]()
            elif step == "z2":
                piece.exchange("z2")
            elif step == "zz":
                piece.exchange("z1")
            else:
                piece.halve(step)
        q, rest, mixed, gd, gu = [have[name] for name in ("q", "r", "mixed", "down", "up")]

        where = qkv_starts(c) + qkv_starts(1 - c)
        moves = []
        for core in (0, 1):
            for side in (0, 1):
                for g in range(3 * pairs):
                    moves.append((((0, 1), (2,))[core], side * quarter, g * PAIR, PAIR,
                                  6 * pairs * core + 3 * pairs * side + g))
        gq = line.do(
            lambda *v: place(x, where, v, quarter, 3 * width, moves), q.keep, q.got, q.other)
        def in_halves(keep, got):
            n = quarter // 2
            out = [pick(keep[:n], got[:n], x), pick(got[:n], keep[:n], x)]
            v = [pick(keep[n:], got[n:], x), pick(got[n:], keep[n:], x)]
            return up32(jnp.concatenate(out, 0)), up32(jnp.concatenate(v, 0)).reshape(-1)

        go, vectors = line.do(in_halves, rest.keep, rest.got)
        token_grad = line.token

        cuts = [vectors[offsets[i]:offsets[i] + quarter] for i in range(6)]
        v_g1, v_b1, v_ob, v_g2, v_b2, v_db = cuts
        v_qv = vectors[offsets[6]:offsets[7]]
        v_ub = vectors[offsets[7]:offsets[7] + ffq]
        return (
            mixed, token_grad, v_g1, v_b1, gq, v_qv, go, v_ob, v_g2, v_b2, gu, v_ub, gd, v_db,
        )

    return per_device


def solution(mesh):
    rows = P(("rep", "shard"), None, None)
    vec, mat = P("shard"), P("shard", None)
    return jax.shard_map(
        build(mesh),
        mesh=mesh,
        in_specs=(rows, rows, P(("rep", "shard")), vec, vec, mat, vec, mat, vec, vec, vec,
                  mat, vec, mat, vec),
        out_specs=(rows, rows, vec, vec, mat, vec, mat, vec, vec, vec, mat, vec, mat, vec),
        check_vma=False,
    )
```

```python
import functools
import math

import jax
import jax.numpy as jnp
from jax import lax
from jax.experimental import pallas as pl
from jax.experimental.pallas import tpu as pltpu
from jax.sharding import PartitionSpec as P

HEAD_DIM = 64
PAIR = 2 * HEAD_DIM
EPSILON = 1e-06
BF = jnp.bfloat16
F32 = jnp.float32
NT = ((1,), (1,))
TN = ((0,), (0,))
VMEM_BYTES = 32 << 20


def up32(values):
    return values.astype(F32)


def flip(axis, size, bit):
    pairs = [(i, i ^ bit) for i in range(size)]
    return lambda values: lax.ppermute(values, axis, pairs)


def pick(first, second, index):
    return jnp.where(index == 0, first, second)


def dot(left, right, contract=((1,), (0,))):
    return lax.dot_general(left, right, (contract, ((), ())), preferred_element_type=F32)


def tie(*values):
    return lax.optimization_barrier(values)


def normalize(values):
    average = jnp.mean(values, -1, keepdims=True)
    centered = values - average
    inverse = lax.rsqrt(jnp.mean(centered * centered, -1, keepdims=True) + EPSILON)
    return centered * inverse, inverse


def norm_back(upstream, normed, inverse, gain):
    scaled = upstream * gain
    return inverse * (
        scaled
        - jnp.mean(scaled, -1, keepdims=True)
        - normed * jnp.mean(scaled * normed, -1, keepdims=True)
    )


def gelu_parts(values):
    phi = 0.5 * (1.0 + lax.erf(values * (1.0 / math.sqrt(2.0))))
    slope = phi + values * jnp.exp(-0.5 * values * values) * (1.0 / math.sqrt(2.0 * math.pi))
    return values * phi, slope


def attend_kernel(seq, tile, raw_ref, out_ref, log_ref):
    n = raw_ref.shape[0]
    lane = lax.broadcasted_iota(jnp.int32, (n, PAIR), 1)
    row = lax.broadcasted_iota(jnp.int32, (n, PAIR), 0)
    keys, values = raw_ref[:, PAIR:2 * PAIR], raw_ref[:, 2 * PAIR:]
    one, zero = jnp.asarray(1, BF), jnp.asarray(0, BF)
    low = jnp.asarray(-1e30, BF)
    mine = [(lane // HEAD_DIM) == h for h in (0, 1)]
    spare = [lane == (1 - h) * HEAD_DIM for h in (0, 1)]
    k_of = [jnp.where(mine[h], keys, jnp.where(spare[h] & (row >= seq), low, zero)) for h in (0, 1)]
    v_of = [jnp.where(mine[h], values, one) for h in (0, 1)]
    jobs = [(t, min(tile, n - t), h) for t in range(0, n, tile) for h in (0, 1)]

    def score(job):
        t, m, h = job
        q = raw_ref[t:t + m, :PAIR] * jnp.asarray(1.0 / math.sqrt(HEAD_DIM), BF)
        q = jnp.where(mine[h][t:t + m], q, jnp.where(spare[h][t:t + m], one, zero))
        return dot(q, k_of[h], NT)

    ahead = 2
    ready = [score(job) for job in jobs[:ahead]]
    for i, (t, m, h) in enumerate(jobs):
        if i + ahead < len(jobs):
            ready.append(score(jobs[i + ahead]))
        s = ready.pop(0)
        top = jnp.max(s, -1, keepdims=True)
        res = dot(jnp.exp(s - top).astype(BF), v_of[h])
        own = slice(h * HEAD_DIM, (h + 1) * HEAD_DIM)
        other = slice((1 - h) * HEAD_DIM, (2 - h) * HEAD_DIM)
        total = res[:, other]
        out_ref[t:t + m, own] = (res[:, own] / total).astype(BF)
        log_ref[t:t + m, own] = top + jnp.log(total)


def attend(raw, seq, images, padded, first, groups):
    spec = pl.BlockSpec((padded, PAIR), lambda i, g: (i, g))
    return pl.pallas_call(
        functools.partial(attend_kernel, seq, 304),
        grid=(images, groups),
        in_specs=[pl.BlockSpec((padded, 3 * PAIR), lambda i, g: (i, first + g))],
        out_specs=[spec, spec],
        out_shape=[
            jax.ShapeDtypeStruct((images * padded, groups * PAIR), BF),
            jax.ShapeDtypeStruct((images * padded, groups * PAIR), F32),
        ],
        compiler_params=pltpu.CompilerParams(vmem_limit_bytes=VMEM_BYTES),
        name="attend",
    )(raw)


def attend_back_kernel(seq, wide, raw_ref, d_ref, log_ref, out_ref, sum_ref, kk_ref, vv_ref, p_ref,
                       s_ref):
    n = raw_ref.shape[0]
    scale = 1.0 / math.sqrt(HEAD_DIM)
    lane = lax.broadcasted_iota(jnp.int32, (n, PAIR), 1)
    zero = jnp.asarray(0, BF)
    gap = jnp.zeros((wide - n, PAIR), BF)

    def stacked(v):
        first = lane < HEAD_DIM
        return jnp.concatenate([jnp.where(first, v, zero), gap, jnp.where(first, zero, v), gap], 0)

    kk_ref[:, :PAIR] = stacked(raw_ref[:, PAIR:2 * PAIR])
    vv_ref[...] = stacked(raw_ref[:, 2 * PAIR:])

    @pl.when((pl.program_id(0) == 0) & (pl.program_id(1) == 0))
    def _():
        lanes = lax.broadcasted_iota(jnp.int32, (2 * wide, PAIR), 1)
        row = lax.broadcasted_iota(jnp.int32, (2 * wide, PAIR), 0)
        row = jnp.where(row >= wide, row - wide, row)
        kk_ref[:, PAIR:] = jnp.where((lanes == 0) & (row >= seq), jnp.asarray(-1e30, BF), zero)

    q = raw_ref[:, :PAIR]
    d = d_ref[...]
    mask = jnp.where(lane == 0, jnp.asarray(1, BF), zero)
    s = dot(jnp.concatenate([q * jnp.asarray(scale, BF), mask], 1), kk_ref[...], NT)
    dp = dot(d, vv_ref[...], NT)
    for h in (0, 1):
        cols = slice(h * wide, (h + 1) * wide)
        p = jnp.exp(s[:, cols] - log_ref[:, h * HEAD_DIM:h * HEAD_DIM + 1])
        dph = dp[:, cols]
        p_ref[:, cols] = p.astype(BF)
        s_ref[:, cols] = (p * (dph - jnp.sum(dph * p, -1, keepdims=True))).astype(BF)
    dk = dot(s_ref[...], q, TN)
    dv = dot(p_ref[...], d, TN)
    first = lane < HEAD_DIM
    for j, value in enumerate((
            dot(s_ref[...], kk_ref[:, :PAIR]) * scale,
            jnp.where(first, dk[:n], dk[wide:wide + n]) * scale,
            jnp.where(first, dv[:n], dv[wide:wide + n]))):
        cols = slice(j * PAIR, (j + 1) * PAIR)
        low = value.astype(BF)
        out_ref[:, cols] = low
        sum_ref[0, :, cols] = jnp.broadcast_to(
            jnp.sum(up32(low), 0, keepdims=True), (sum_ref.shape[1], PAIR))


def attend_back(raw, d_att, logs, seq, images, padded, start, groups):
    wide = -(-padded // 128) * 128
    one = pl.BlockSpec((padded, PAIR), lambda i, g: (i, start + g))
    log = pl.BlockSpec((padded, PAIR), lambda i, g: (i, g))
    three = pl.BlockSpec((padded, 3 * PAIR), lambda i, g: (i, start + g))
    cols = groups * 3 * PAIR
    return pl.pallas_call(
        functools.partial(attend_back_kernel, seq, wide),
        grid=(images, groups),
        in_specs=[three, one, log],
        out_specs=[pl.BlockSpec((padded, 3 * PAIR), lambda i, g: (i, g)),
                   pl.BlockSpec((1, 8, 3 * PAIR), lambda i, g: (i, 0, g))],
        out_shape=[jax.ShapeDtypeStruct((raw.shape[0], cols), BF),
                   jax.ShapeDtypeStruct((images, 8, cols), F32)],
        scratch_shapes=[
            pltpu.VMEM((2 * wide, 2 * PAIR), BF),
            pltpu.VMEM((2 * wide, PAIR), BF),
            pltpu.VMEM((padded, 2 * wide), BF),
            pltpu.VMEM((padded, 2 * wide), BF),
        ],
        compiler_params=pltpu.CompilerParams(vmem_limit_bytes=VMEM_BYTES),
        name="attend_back",
    )(raw, d_att, logs)


TILE = 592
WIDE = 512


def whole(array):
    return pl.BlockSpec(array.shape, lambda *_: (0,) * array.ndim)


def params():
    return pltpu.CompilerParams(vmem_limit_bytes=VMEM_BYTES)


def spread_kernel(size, starts, c_ref, w_ref, own_ref, other_ref):
    rows = w_ref.shape[0]
    wide = own_ref.shape[1] // size
    for core in (0, 1):
        @pl.when(c_ref[0] == core)
        def _(core=core):
            for out_ref, columns in ((own_ref, starts[core]), (other_ref, starts[1 - core])):
                for i, start in enumerate(columns):
                    row, col = i // wide * rows, i % wide * size
                    out_ref[row:row + rows, col:col + size] = w_ref[:, start:start + size]


def spread(core, w, starts, size, blocks):
    count = len(starts[0])
    out = jax.ShapeDtypeStruct((w.shape[0] * blocks, count // blocks * size), w.dtype)
    return pl.pallas_call(
        functools.partial(spread_kernel, size, starts),
        grid_spec=pltpu.PrefetchScalarGridSpec(
            num_scalar_prefetch=1, grid=(1,), in_specs=[whole(w)], out_specs=[whole(out)] * 2),
        out_shape=[out] * 2, compiler_params=params(), name="spread")(core, w)


def row_mask(tile, seq):
    return lax.broadcasted_iota(jnp.int32, (TILE, 1), 0) + tile * TILE < seq


def near_first(value, y):
    half = value.shape[1] // 2
    a, b = value[:, :half], value[:, half:]
    return jnp.concatenate([jnp.where(y == 0, a, b), jnp.where(y == 0, b, a)], 1)


def column_sum(value):
    return jnp.sum(value, 0, keepdims=True)


def rows_call(kernel, scalars, arrays, vectors, outs, sums, name):
    images = arrays[-1].shape[-3]
    padded = max(v.shape[-2] for v in (*arrays, *outs))

    def spec(v):
        if len(v.shape) == 3:
            return pl.BlockSpec((1, TILE, v.shape[-1]), lambda i, t, s: (i, t, 0))
        return pl.BlockSpec((2, 1, TILE, v.shape[-1]), lambda i, t, s: (0, i, t, 0))

    width = arrays[0].shape[-1]
    more = [jax.ShapeDtypeStruct((8, width), F32)] if sums else []
    return pl.pallas_call(
        kernel,
        grid_spec=pltpu.PrefetchScalarGridSpec(
            num_scalar_prefetch=1, grid=(images, -(-padded // TILE)),
            in_specs=[*map(spec, arrays), *map(whole, vectors)],
            out_specs=[*map(spec, outs), *map(whole, more)]),
        out_shape=[*outs, *more],
        compiler_params=params(),
        name=name,
    )(scalars, *arrays, *vectors)


def enter_kernel(seq, s_ref, own_ref, other_ref, grad_ref, grad2_ref, gain_ref, shift_ref,
                 norm_ref, out_ref):
    k = pl.program_id(0)
    ok = row_mask(pl.program_id(2), seq)
    mine = k == s_ref[1]
    unit, _ = normalize(up32(jnp.where(mine, own_ref[0], other_ref[0])))
    normed = jnp.where(ok, near_first(unit * gain_ref[...] + shift_ref[...], s_ref[0]), 0.0)
    norm_ref[0, 0] = normed.astype(BF)
    valid = s_ref[2 + k * pl.num_programs(1) + pl.program_id(1)]
    grad = up32(jnp.where(mine, grad_ref[0], grad2_ref[0]))
    out_ref[0, 0] = jnp.where(ok & (valid != 0), grad * up32(valid), 0.0).astype(BF)


def enter(scalars, own, other, grad, grad2, gain, shift, padded):
    images, seq, width = own.shape
    spec = pl.BlockSpec((1, TILE, width), lambda k, i, t, s: (i, t, 0))
    out = jax.ShapeDtypeStruct((2, images, padded, width), BF)
    out_spec = pl.BlockSpec((1, 1, TILE, width), lambda k, i, t, s: (k, i, t, 0))
    return pl.pallas_call(
        functools.partial(enter_kernel, seq),
        grid_spec=pltpu.PrefetchScalarGridSpec(
            num_scalar_prefetch=1, grid=(2, images, -(-padded // TILE)),
            in_specs=[spec] * 4 + [whole(gain), whole(shift)], out_specs=[out_spec] * 2),
        out_shape=[out, out],
        compiler_params=params(),
        name="enter",
    )(scalars, own, other, grad, grad2, gain, shift)


def middle_kernel(seq, s_ref, x_ref, parts_ref, add_ref, gain_ref, shift_ref, mid_ref, norm_ref):
    ok = row_mask(pl.program_id(1), seq)
    middle = up32(x_ref[0]) + (up32(parts_ref[0, 0]) + up32(parts_ref[1, 0])) + add_ref[...]
    middle = jnp.where(ok, middle, 0.0)
    mid_ref[0] = middle
    unit, _ = normalize(middle)
    normed = jnp.where(ok, near_first(unit * gain_ref[...] + shift_ref[...], s_ref[0]), 0.0)
    for k in (0, 1):
        norm_ref[k, 0] = normed.astype(BF)


def start_sums(sum_ref):
    @pl.when((pl.program_id(0) == 0) & (pl.program_id(1) == 0))
    def _():
        sum_ref[...] = jnp.zeros_like(sum_ref)


def back_middle_kernel(seq, s_ref, parts_ref, mid_ref, grad_ref, gain_ref, d_ref, low_ref, sum_ref):
    i = pl.program_id(0)
    ok = row_mask(pl.program_id(1), seq)
    unit, inverse = normalize(mid_ref[0])
    h = near_first(up32(parts_ref[0, 0]) + up32(parts_ref[1, 0]), s_ref[0])
    h = jnp.where(ok, h, 0.0)
    unit = jnp.where(ok, unit, 0.0)
    valid = s_ref[1 + i]
    dy = jnp.where(ok & (valid != 0), up32(grad_ref[0]) * up32(valid), 0.0)
    d_middle = jnp.where(ok, dy + norm_back(h, unit, inverse, gain_ref[...]), 0.0)
    low = d_middle.astype(BF)
    d_ref[0] = d_middle
    for k in (0, 1):
        low_ref[k, 0] = low
    start_sums(sum_ref)
    for row, value in enumerate((h * unit, h, up32(low), up32(dy.astype(BF)))):
        sum_ref[row:row + 1, :] += column_sum(value)


def leave_kernel(seq, s_ref, parts_ref, x_ref, mid_ref, gain_ref, d_ref, sum_ref):
    ok = row_mask(pl.program_id(1), seq)
    unit, inverse = normalize(up32(x_ref[0]))
    h = near_first(up32(parts_ref[0, 0]) + up32(parts_ref[1, 0]), s_ref[0])
    h = jnp.where(ok, h, 0.0)
    d_ref[0] = (mid_ref[0] + norm_back(h, unit, inverse, gain_ref[...])).astype(BF)
    start_sums(sum_ref)
    for row, value in enumerate((jnp.where(ok, h * unit, 0.0), h)):
        sum_ref[row:row + 1, :] += column_sum(value)


def place_kernel(count, moves, where_ref, *refs):
    ins, out_ref = refs[:count], refs[count]
    x = where_ref[0]
    for numbers, row, col, size, entry in moves:
        rows = slice(row, row + out_ref.shape[0])
        a, b = [up32(ins[i][rows, col:col + size]) for i in (numbers * 2)[:2]]
        start = pl.multiple_of(where_ref[1 + entry], 128)
        out_ref[:, pl.ds(start, size)] = jnp.where(x == 0, a, b)


def place(x, where, inputs, rows, width, moves):
    out = jax.ShapeDtypeStruct((rows, width), F32)
    return pl.pallas_call(
        functools.partial(place_kernel, len(inputs), moves),
        grid_spec=pltpu.PrefetchScalarGridSpec(
            num_scalar_prefetch=1, grid=(1,), in_specs=[whole(v) for v in inputs],
            out_specs=whole(out)),
        out_shape=out,
        compiler_params=params(),
        name="place",
    )(jnp.stack([jnp.asarray(w, jnp.int32) for w in [x, *where]]), *inputs)


def halves_kernel(s_ref, *refs):
    out_ref = refs[-1]
    h = pl.program_id(0) % 2
    for k in range(len(refs) // 2):
        @pl.when(pl.program_id(0) // 2 == k)
        def _(keep_ref=refs[2 * k], got_ref=refs[2 * k + 1]):
            out_ref[...] = up32(jnp.where(s_ref[0] == h, keep_ref[...], got_ref[...]))


def halves(x, pairs, rows):
    width = pairs[0].shape[1]
    spec = pl.BlockSpec((rows, width), lambda i, s: (0, 0))
    return pl.pallas_call(
        halves_kernel,
        grid_spec=pltpu.PrefetchScalarGridSpec(
            num_scalar_prefetch=1, grid=(len(pairs),), in_specs=[spec] * len(pairs),
            out_specs=pl.BlockSpec((rows, width), lambda i, s: (i, 0))),
        out_shape=jax.ShapeDtypeStruct((len(pairs) * rows, width), F32),
        compiler_params=params(),
        name="halves",
    )(x, *pairs)


def pack_kernel(*refs):
    at = 0
    for ref in refs[:-1]:
        refs[-1][:, at:at + ref.shape[1]] = up32(ref[...])
        at += ref.shape[1]


def pack(*vectors):
    vectors = [v[None] for v in vectors]
    out = jax.ShapeDtypeStruct((1, sum(v.shape[1] for v in vectors)), F32)
    return pl.pallas_call(
        pack_kernel, grid=(1,), in_specs=[whole(v) for v in vectors], out_specs=whole(out),
        out_shape=out, compiler_params=params(), name="pack")(*vectors)


def small_kernel(offsets, quarter, parts, pairs, c_ref, all_ref, vec_ref, bias_ref, upb_ref):
    c = c_ref[0]

    def of(shard, start, size):
        row = shard % 2 * 2 + shard // 2
        return all_ref[row:row + 1, start:start + size]

    for row, at in enumerate(offsets[:6]):
        for q in range(4):
            vec_ref[row:row + 1, q * quarter:(q + 1) * quarter] = of(q, at, quarter)
    qv, up = offsets[6:]

    def block(b):
        return of(b // 2, qv + b % 2 * quarter, quarter)

    for side in (0, 1):
        for part in range(3):
            if part == 1:
                value = jnp.zeros((1, quarter), F32)
            else:
                b = 2 * part + 2 * side
                value = jnp.where(c == 0, block(b), block(b + 1))
            for g in range(pairs):
                to = ((side * pairs + g) * 3 + part) * PAIR
                bias_ref[:, to:to + PAIR] = value[:, g * PAIR:(g + 1) * PAIR]
    fp = upb_ref.shape[1] // 2 // parts
    for k in range(parts):
        for side in (0, 1):
            to = (2 * k + side) * fp
            start = up + k * fp
            upb_ref[:, to:to + fp] = jnp.where(
                c == 0, of(2 * side, start, fp), of(2 * side + 1, start, fp))


def small_call(core, gathered, offsets, quarter, ffq, parts, pairs):
    shapes = [jax.ShapeDtypeStruct(s, F32)
              for s in ((8, 4 * quarter), (1, 6 * quarter), (1, 2 * ffq))]
    return pl.pallas_call(
        functools.partial(small_kernel, offsets, quarter, parts, pairs),
        grid_spec=pltpu.PrefetchScalarGridSpec(
            num_scalar_prefetch=1, grid=(1,), in_specs=[whole(gathered)],
            out_specs=[whole(s) for s in shapes]),
        out_shape=shapes,
        compiler_params=params(),
        name="small",
    )(core, gathered)


def vectors_kernel(offsets, quarter, parts, pairs, c_ref, one_ref, two_ref, low_ref, high_ref, *refs):
    ups, out_ref = refs[:parts], refs[parts]
    c = c_ref[0]
    rows = ((one_ref, 0), (one_ref, 1), (two_ref, 2), (two_ref, 0), (two_ref, 1), (two_ref, 3))
    qv, up = offsets[6:]

    def sums(ref, part):
        total = jnp.sum(ref[:, 0, :], 0, keepdims=True)
        return jnp.concatenate(
            [total[:, (3 * g + part) * PAIR:(3 * g + part + 1) * PAIR] for g in range(pairs)], 1)

    table = [[sums(ref, part) for part in (0, 2)] for ref in (low_ref, high_ref)]
    fp = ups[0].shape[1] // 2
    for core in (0, 1):
        for side in (0, 1):
            to = 2 * core + side
            shard = 2 * side + core
            for (ref, row), at in zip(rows, offsets[:6]):
                out_ref[to:to + 1, at:at + quarter] = (
                    ref[row:row + 1, shard * quarter:(shard + 1) * quarter])
            for h in (0, 1):
                block = 2 * shard + h
                value = table[block % 4 // 2][block // 4]
                out_ref[to:to + 1, qv + h * quarter:qv + (h + 1) * quarter] = jnp.where(
                    c == block % 2, value, 0.0)
            for k, ref in enumerate(ups):
                out_ref[to:to + 1, up + k * fp:up + (k + 1) * fp] = jnp.where(
                    c == core, ref[:, side * fp:(side + 1) * fp], 0.0)


def vectors_call(core, one, two, low, high, ups, offsets, quarter, width, pairs):
    out = jax.ShapeDtypeStruct((4, width), F32)
    ins = [one, two, low, high, *ups]
    return pl.pallas_call(
        functools.partial(vectors_kernel, offsets, quarter, len(ups), pairs),
        grid_spec=pltpu.PrefetchScalarGridSpec(
            num_scalar_prefetch=1, grid=(1,), in_specs=[whole(v) for v in ins],
            out_specs=whole(out)),
        out_shape=out,
        compiler_params=params(),
        name="vectors",
    )(core, *ins)


def feed_kernel(s_ref, n2_ref, do_ref, own_ref, other_ref, ua_ref, ub_ref, near_ref, da_ref,
                db_ref, bias_ref, h_ref, act_ref, keep_ref, send_ref, hsum_ref,
                sum_ref, up_ref, down_ref, acc_ref):
    x, y = s_ref[0], s_ref[1]
    j = pl.program_id(0)
    steps = pl.num_programs(0)
    half = steps // 2
    wide = up_ref.shape[1]
    quarter = own_ref.shape[0]
    up_ref[:quarter, :] = own_ref[...]
    up_ref[quarter:2 * quarter, :] = other_ref[...]
    a, b = ua_ref[...], ub_ref[...]
    up_ref[2 * quarter:3 * quarter, :] = jnp.where(x == 0, a, b)
    up_ref[3 * quarter:, :] = jnp.where(x == 0, b, a)
    near = j // half == y

    @pl.when(near)
    def _():
        down_ref[...] = near_ref[...]

    @pl.when(jnp.logical_not(near))
    def _():
        down_ref[...] = jnp.where((x == 0) == (j % half == 0), da_ref[...], db_ref[...])

    n2, do = n2_ref[...], do_ref[...]
    act, slope = gelu_parts(dot(n2, up_ref[...]) + bias_ref[...])
    act = act.astype(BF)
    act_ref[...] = act
    d_pre = (dot(do, down_ref[...], NT) * slope).astype(BF)
    sum_ref[...] = jnp.sum(up32(d_pre), 0, keepdims=True)
    gd = dot(act, do, TN).astype(BF)
    at_rows = pl.ds(pl.multiple_of(j % half * wide, wide), wide)

    @pl.when(near)
    def _():
        keep_ref[at_rows, :] = gd

    @pl.when(jnp.logical_not(near))
    def _():
        send_ref[at_rows, :] = gd

    gu = dot(n2, d_pre, TN).astype(BF)
    cols = pl.ds(pl.multiple_of(j * wide, wide), wide)
    keep_ref[half * wide:, cols] = gu[:2 * quarter]
    send_ref[half * wide:, cols] = gu[2 * quarter:]

    @pl.when(j == 0)
    def _():
        acc_ref[...] = h_ref[...]

    acc_ref[...] += dot(d_pre, up_ref[...], NT)

    @pl.when(j == steps - 1)
    def _():
        hsum_ref[...] = acc_ref[...].astype(BF)


def feed(scalars, n2, do, near_up, a, b, down, bias, h, k, wide=256):
    both, width = n2.shape
    quarter = width // 4
    cols = bias.shape[1]
    half = cols // 2 // wide
    parts = near_up.shape[0] // 2 // quarter
    n2_spec = whole(n2)
    piece = jax.ShapeDtypeStruct((cols // 2 + width // 2, width), BF)
    low = jax.ShapeDtypeStruct((both, width), BF)

    def near(j, s):
        return (k * half + jnp.where(j // half == s[1], j % half, 0), 0)

    return pl.pallas_call(
        feed_kernel,
        grid_spec=pltpu.PrefetchScalarGridSpec(
            num_scalar_prefetch=1, grid=(2 * half,),
            in_specs=[
                n2_spec, n2_spec,
                pl.BlockSpec((quarter, wide), lambda j, s: (k, j)),
                pl.BlockSpec((quarter, wide), lambda j, s: (parts + k, j)),
                pl.BlockSpec((quarter, wide), lambda j, s: (0, j)),
                pl.BlockSpec((quarter, wide), lambda j, s: (0, j)),
                pl.BlockSpec((wide, width), near),
                pl.BlockSpec((wide, width), lambda j, s: (quarter // wide, 0)),
                pl.BlockSpec((wide, width), lambda j, s: (quarter // wide, 0)),
                pl.BlockSpec((1, wide), lambda j, s: (0, j)),
                whole(h)],
            out_specs=[
                pl.BlockSpec((both, wide), lambda j, s: (0, j)),
                whole(piece), whole(piece),
                whole(low),
                pl.BlockSpec((1, wide), lambda j, s: (0, j))],
            scratch_shapes=[pltpu.VMEM((width, wide), BF), pltpu.VMEM((wide, width), BF),
                            pltpu.VMEM((both, width), F32)]),
        out_shape=[jax.ShapeDtypeStruct((both, cols), BF), piece, piece, low,
                   jax.ShapeDtypeStruct((1, cols), F32)],
        compiler_params=pltpu.CompilerParams(vmem_limit_bytes=58 << 20),
        name="feed",
    )(scalars, n2, do, near_up, near_up, a, b, down, a, b, bias, h)


def halve_kernel(sizes, s_ref, keep_ref, got_ref, mine_ref, theirs_ref):
    at = 0
    for i, size in enumerate(sizes):
        n = size // 2
        for bit, out_ref in ((s_ref[i], mine_ref), (1 - s_ref[i], theirs_ref)):
            rows = pl.ds(pl.multiple_of(at + bit * n, 16), n)
            out_ref[at // 2:at // 2 + n, :] = added(keep_ref[rows, :], got_ref[rows, :])
        at += size


def add_kernel(keep_ref, got_ref, out_ref):
    out_ref[...] = added(keep_ref[...], got_ref[...])


def other_kernel(sizes, cross, s_ref, keep_ref, got_ref, out_ref):
    at, to = 0, 0
    for size, crosses in zip(sizes, cross):
        if crosses:
            out_ref[to:to + size, :] = jnp.where(
                s_ref[0] == 0, got_ref[at:at + size, :], keep_ref[at:at + size, :])
            to += size
        at += size


def join_kernel(sizes, s_ref, keep_ref, got_ref, out_ref):
    at = 0
    for size in sizes:
        rows = slice(at, at + size)
        keep, got = keep_ref[rows, :], got_ref[rows, :]
        out_ref[2 * at:2 * at + size, :] = jnp.where(s_ref[0] == 0, keep, got)
        out_ref[2 * at + size:2 * (at + size), :] = jnp.where(s_ref[0] == 0, got, keep)
        at += size


def columns_call(kernel, scalars, arrays, rows, block, outs, name):
    cols = arrays[0].shape[1]
    width = WIDE if cols % WIDE == 0 else cols // 2
    spec = pl.BlockSpec((rows, width), lambda j, *_: (block, j))
    out_specs = [pl.BlockSpec((n, width), lambda j, *_: (0, j)) for n in outs]
    return pl.pallas_call(
        kernel,
        grid_spec=pltpu.PrefetchScalarGridSpec(
            num_scalar_prefetch=len(scalars), grid=(cols // width,),
            in_specs=[spec] * len(arrays), out_specs=out_specs),
        out_shape=[jax.ShapeDtypeStruct((n, cols), BF) for n in outs],
        compiler_params=params(),
        name=name,
    )(*scalars, *arrays)


def pair_kernel(n_ref, a_ref, b_ref, out_ref):
    for j, ref in enumerate((a_ref, b_ref)):
        @pl.when(pl.program_id(0) == j)
        def _(ref=ref):
            out_ref[...] = dot(n_ref[...], ref[...], TN).astype(BF)


def pair_sums(n, a, b, side):
    rows, half = n.shape[0], n.shape[1] // 2
    cols = a.shape[1]
    return pl.pallas_call(
        pair_kernel,
        grid=(2,),
        in_specs=[pl.BlockSpec((rows, half), lambda j: (0, side)), whole(a), whole(b)],
        out_specs=pl.BlockSpec((half, cols), lambda j: (j, 0)),
        out_shape=jax.ShapeDtypeStruct((2 * half, cols), BF),
        compiler_params=params(),
        name="pair_sums",
    )(n, a, b)


def back_in_kernel(a_ref, b_ref, w_ref, out_ref):
    cut = a_ref.shape[1]
    total = dot(a_ref[...], w_ref[:, :cut], NT) + dot(b_ref[...], w_ref[:, cut:], NT)
    out_ref[...] = total.astype(BF)


def back_in(a, b, w, wide=512):
    out = jax.ShapeDtypeStruct((a.shape[0], w.shape[0]), BF)
    return pl.pallas_call(
        back_in_kernel,
        grid=(w.shape[0] // wide,),
        in_specs=[whole(a), whole(b), pl.BlockSpec((wide, w.shape[1]), lambda j: (j, 0))],
        out_specs=pl.BlockSpec((a.shape[0], wide), lambda j: (0, j)),
        out_shape=out,
        compiler_params=params(),
        name="back_in",
    )(a, b, w)


def out_sums_kernel(s_ref, a_ref, b_ref, d_ref, send_ref, keep_ref):
    d = d_ref[...]
    for j, out_ref in enumerate((send_ref, keep_ref)):
        for y, ref in enumerate((a_ref, b_ref)):
            @pl.when((pl.program_id(0) == j) & (s_ref[0] == (y ^ 1 ^ j)))
            def _(ref=ref, out_ref=out_ref):
                out_ref[...] = dot(ref[...], d, TN).astype(BF)


def out_sums(scalars, a, b, d):
    out = jax.ShapeDtypeStruct((a.shape[1], d.shape[1]), BF)
    return pl.pallas_call(
        out_sums_kernel,
        grid_spec=pltpu.PrefetchScalarGridSpec(
            num_scalar_prefetch=1, grid=(2,), in_specs=[whole(a), whole(b), whole(d)],
            out_specs=[whole(out)] * 2),
        out_shape=[out] * 2,
        compiler_params=params(),
        name="out_sums",
    )(scalars, a, b, d)


def feed_out_kernel(s_ref, one_ref, two_ref, down_ref, near_ref, a_ref, b_ref, out_ref):
    x, y = s_ref[0], s_ref[1]
    n = near_ref.shape[0]
    total = dot(one_ref[...], down_ref[...])
    total += dot(two_ref[:, pl.ds(pl.multiple_of(y * n, n), n)], near_ref[...])
    a, b = a_ref[...], b_ref[...]
    for i, w in enumerate((jnp.where(x == 0, a, b), jnp.where(x == 0, b, a))):
        start = pl.multiple_of((1 - y) * n + i * (n // 2), n // 2)
        total += dot(two_ref[:, pl.ds(start, n // 2)], w)
    out_ref[...] = total.astype(BF)


def feed_out(scalars, one, two, down, near, a, b, k, wide=512):
    rows, cols = one.shape[0], down.shape[1]
    n = two.shape[1] // 2
    return pl.pallas_call(
        feed_out_kernel,
        grid_spec=pltpu.PrefetchScalarGridSpec(
            num_scalar_prefetch=1, grid=(cols // wide,),
            in_specs=[
                whole(one), whole(two), pl.BlockSpec((down.shape[0], wide), lambda j, s: (0, j)),
                pl.BlockSpec((n, wide), lambda j, s: (k, j)),
                pl.BlockSpec((n // 2, wide), lambda j, s: (1, j)),
                pl.BlockSpec((n // 2, wide), lambda j, s: (1, j))],
            out_specs=pl.BlockSpec((rows, wide), lambda j, s: (0, j))),
        out_shape=jax.ShapeDtypeStruct((rows, cols), BF),
        compiler_params=params(),
        name="feed_out",
    )(scalars, one, two, down, near, a, b)


ORDER = (
    "swap_h", "back_mid", "swap_d", "m0.x", "to_heads", "out_send", "attend_0", "attend_1", "m0.z1",
    "q_send", "m1.x", "q_keep", "to_input", "swap_in", "m0.z2", "leave", "small_sums", "m1.z1",
    "to_mixed", "q.x", "small_y", "m0.back", "m1.z2", "rest", "q.z1", "m0.join", "r.x", "m1.back",
    "q.z2", "r.zz", "m1.join", "m0.over", "q.back", "r.z2", "q.join", "m1.over", "rest_back",
    "q.over", "swap_mixed", "grad_down", "mixed", "grad_up",
)


class Line:
    def __init__(self, token):
        self.token = token

    def tie(self, *values):
        *values, self.token = lax.optimization_barrier((*values, self.token))
        return values[0] if len(values) == 1 else values

    def do(self, step, *values):
        values = self.tie(*values)
        out = step(*values) if isinstance(values, list) else step(values)
        return self.tie(*out) if isinstance(out, (list, tuple)) else self.tie(out)


def added(keep, got):
    return (up32(keep) + up32(got)).astype(BF)


class Sum:
    def __init__(self, line, swaps, at, got, keep, sizes, cross, block=0):
        self.line, self.swaps, self.at, self.cross = line, swaps, at, cross
        self.got, self.keep, self.sizes, self.block = got, keep, sizes, block

    def run(self, kernel, bits, outs, name):
        scalars = [jnp.stack(bits).astype(jnp.int32)] if bits else []
        out = self.line.do(
            lambda keep, got: columns_call(
                kernel, scalars, [keep, got], sum(self.sizes), self.block, outs, name),
            self.keep, self.got)
        self.block = 0
        return out

    def halve(self, axis):
        bits = [self.at["cross" if cross and axis == "x" else axis] for cross in self.cross]
        n = sum(self.sizes) // 2
        self.keep, theirs = self.run(
            functools.partial(halve_kernel, self.sizes), bits, [n, n], "halve")
        self.sizes = [n // 2 for n in self.sizes]
        self.got = self.swaps[axis](theirs)

    def add(self):
        self.keep = self.run(add_kernel, [], [sum(self.sizes)], "add")

    def exchange(self, axis):
        self.add()
        self.got = self.swaps[axis](self.keep)

    def back(self):
        self.add()
        for swap in self.swaps["rest"]:
            self.got = swap(self.keep)
            self.add()
        self.got = self.swaps["z1"](self.keep)

    def join(self):
        self.keep = self.run(
            functools.partial(join_kernel, self.sizes), [self.at["z1"]], [2 * sum(self.sizes)], "join")
        self.sizes = [2 * n for n in self.sizes]
        self.got = self.swaps["x"](self.keep)

    def land(self):
        self.got = self.line.tie(self.got)

    def cross_over(self):
        rows = sum(n for n, cross in zip(self.sizes, self.cross) if cross)
        self.keep, self.got = self.line.tie(self.keep, self.got)
        other = self.run(
            functools.partial(other_kernel, self.sizes, self.cross), [self.at["x"]], [rows], "other")
        self.other = self.swaps["core"](other)


def build(mesh):
    reps = mesh.shape["rep"]
    shards = mesh.shape["shard"]
    y_swap = flip("shard", shards, 2)
    cores = [[2 * i, 2 * i + 1] for i in range(shards // 2)]
    bits = [1 << i for i in range(reps.bit_length() - 1)]
    rep_swap = {b: flip("rep", reps, b) for b in bits}

    def core_swap(values):
        return lax.all_to_all(values, "shard", 0, 0, axis_index_groups=cores, tiled=True)

    swaps = {"core": flip("shard", shards, 1), "y": y_swap, "x": rep_swap[bits[0]], "z1": rep_swap[bits[1]],
             "z2": rep_swap[bits[2]], "rest": [rep_swap[b] for b in bits[3:]]}

    def per_device(
        tokens, out_grad, valid, attn_gain, attn_shift, qkv_w, qv_b, out_w, out_b,
        mlp_gain, mlp_shift, up_w, up_b, down_w, down_b,
    ):
        images, seq, width = tokens.shape
        ff = up_w.shape[1]
        quarter = width // shards
        half = width // 2
        ffq = ff // shards
        padded = -(-seq // 16) * 16
        rows = images * padded
        shard = lax.axis_index("shard")
        rep = lax.axis_index("rep")
        y, c = shard // 2, shard % 2
        x = rep % 2
        at = {"x": x, "z1": (rep // 2) % 2, "z2": (rep // 4) % 2, "cross": x ^ c}
        pairs = quarter // PAIR
        parts = 2
        fp = ffq // parts
        core = c[None].astype(jnp.int32)
        scalars = jnp.concatenate([y[None], valid]).astype(jnp.int32)
        place_at = jnp.stack([x, y]).astype(jnp.int32)

        def qkv_starts(core):
            return [part * width + (2 * side + core) * quarter + g * PAIR
                    for side in (0, 1) for g in range(pairs) for part in range(3)]

        def up_starts(core):
            return [(2 * side + core) * ffq + k * fp for k in range(parts) for side in (0, 1)]

        def by_x(v):
            n = v.shape[0] // 2
            return lax.dynamic_slice_in_dim(v, x * n, n, 0)

        def in_order(got, swapped):
            return [pick(got, swapped, x), pick(swapped, got, x)]

        line = Line(valid)
        core_permute = swaps["core"]

        def for_core(v, which):
            n = v.shape[0] // 2
            return lax.dynamic_slice_in_dim(v, which * n, n, 0)

        def by_core(own, other):
            return [pick(own, other, c), pick(other, own, c)]

        tokens2, grad2 = core_permute(tokens), core_permute(out_grad)
        own_qkv, give = line.do(
            lambda w: spread(core, w, [qkv_starts(0), qkv_starts(1)], PAIR, 1), qkv_w)
        other_qkv = core_permute(give)
        own_up, give = line.do(
            lambda w: spread(core, w, [up_starts(0), up_starts(1)], fp, parts), up_w)
        other_up = core_permute(give)
        far = y_swap(line.do(lambda a, b: pick(a, b, x ^ c), own_qkv, other_qkv))
        small = line.do(pack, attn_gain, attn_shift, out_b, mlp_gain, mlp_shift, down_b, qv_b, up_b,
                        jnp.pad(up32(valid), (0, 128 - images)))
        offsets = [i * quarter for i in range(7)] + [8 * quarter]
        far_small = y_swap(small)
        near_up = line.do(
            lambda a, b: jnp.concatenate(by_core(a, b), 0), own_up, other_up)
        out_w = line.tie(out_w)
        far_out = y_swap(out_w)

        def far_part(k):
            def step(a, w):
                at = (parts * x + k) * quarter
                return jnp.concatenate([
                    lax.dynamic_slice_in_dim(a, at, quarter, 0), by_x(w[k * fp:(k + 1) * fp])], 0)

            return y_swap(line.do(step, near_up, down_w))

        far_mlp, far_mlp2 = [far_part(0)], []
        far = line.tie(far)
        far2 = swaps["x"](far)
        small = line.do(
            lambda a, b: jnp.concatenate([pick(a, b, y), pick(b, a, y)] * 2, 0), small, far_small)
        small = line.do(core_swap, small)
        tokens2, grad2 = line.tie(tokens2, grad2)
        vec, bias, upb = line.do(
            lambda v: small_call(core, v, offsets, quarter, ffq, parts, pairs), small)
        g1, b1, ob, g2, b2, db = [vec[i:i + 1] for i in range(6)]

        def shaped(dtype, *lead):
            return jax.ShapeDtypeStruct((*lead, images, padded, width), dtype)

        def cube(v):
            return v.reshape(2, images, padded, width)

        def flat(v):
            return v.reshape(2 * rows, width)

        def kernel(body):
            return functools.partial(body, seq)

        both = jnp.stack([pick(small[2 * k], small[2 * k + 1], y)[-128:images - 128] for k in (0, 1)])
        normed1, d_out = line.do(
            lambda *v: enter(
                jnp.concatenate([jnp.stack([y, c]), both.reshape(-1).astype(jnp.int32)]).astype(
                    jnp.int32), *v, padded),
            tokens, tokens2, out_grad, grad2, g1, b1)
        normed1, d_out = flat(normed1), flat(d_out)
        far_mlp.append(far_part(1))
        far2 = line.tie(far2)
        qkv_full = line.do(
            lambda a, o, b, d: jnp.concatenate(
                [*by_core(a, o), *in_order(b, d)], 0), own_qkv, other_qkv, far, far2)
        raw = line.do(
            lambda n, w, b: (dot(n, w) + b).astype(BF), normed1, qkv_full, bias)
        far_out = line.tie(far_out)

        def attention(first):
            return line.do(lambda v: attend(v, seq, 2 * images, padded, first, pairs), raw)

        def by_y(near, far):
            return [pick(near, far, y), pick(far, near, y)]

        attended, logs = [None] * 2, [None] * 2
        attended[0], logs[0] = attention(0)
        out_full = line.do(lambda a, b: jnp.concatenate(by_y(a, b), 0), out_w, far_out)
        far_mlp[0] = line.tie(far_mlp[0])
        far_mlp2.append(swaps["x"](far_mlp[0]))
        attended[1], logs[1] = attention(pairs)
        branch = line.do(
            lambda a, b, w: (dot(a, w[:quarter]) + dot(b, w[quarter:])).astype(BF),
            *attended, out_full)
        branch = line.do(core_swap, branch)
        middle, normed2 = line.do(
            lambda a, p, *v: rows_call(
                kernel(middle_kernel), scalars, [a, cube(p)], v, [shaped(F32), shaped(BF, 2)],
                False, "middle"),
            tokens, branch, ob, g2, b2)
        normed2 = line.do(core_swap, flat(normed2))
        far_mlp[1] = line.tie(far_mlp[1])
        far_mlp2.append(swaps["x"](far_mlp[1]))

        def tn(a, b):
            return dot(a, b, TN).astype(BF)

        def of_y(v):
            n = v.shape[0] // 2
            return [lax.dynamic_slice_in_dim(v, side * n, n, 0) for side in (1 - y, y)]

        def start(got, keep, sizes, cross, block=0):
            return Sum(line, swaps, at, got, keep, sizes, cross, block)

        n = fp // 2

        def whole_up(a, b, d):
            return jnp.concatenate(
                [a[:quarter], a[parts * quarter:(parts + 1) * quarter],
                 *in_order(b[:quarter], d[:quarter])], 0)

        def whole_down(k):
            def step(near, a, b):
                near, (a, b) = near[k * fp:(k + 1) * fp], in_order(a[quarter:], b[quarter:])
                return jnp.concatenate(
                    [pick(near[:n], a, y), pick(near[n:], b, y),
                     pick(a, near[:n], y), pick(b, near[n:], y)], 0)

            return line.do(step, down_w, far_mlp[k], far_mlp2[k])

        up = line.do(whole_up, near_up, far_mlp[0], far_mlp2[0])

        def forward(n, w, b):
            act, slope = gelu_parts(dot(n, w) + b)
            return act.astype(BF), slope

        act, slope = line.do(forward, normed2, up, upb[:, :2 * fp])
        d_send, d_keep = line.do(of_y, line.do(tn, act, d_out))
        down = whole_down(0)

        def backward(d, w, sl):
            d_pre = (dot(d, w, NT) * sl).astype(BF)
            return d_pre, jnp.sum(up32(d_pre), 0, keepdims=True)

        d_pre, up_sum = line.do(backward, d_out, down, slope)
        far_mlp2[1] = line.tie(far_mlp2[1])
        m_got = y_swap(line.do(
            lambda n, d, v: jnp.concatenate([v, tn(n[:, half:], d)], 0), normed2, d_pre, d_send))
        m_keep = line.do(
            lambda n, d, v: jnp.concatenate([v, tn(n[:, :half], d)], 0), normed2, d_pre, d_keep)
        m0 = start(m_got, m_keep, [fp, half], [False, True])
        h = line.do(lambda d, w: dot(d, w, NT), d_pre, up)
        act2, keep, send, h, up_sum2 = line.do(
            lambda *v: feed(place_at, *v, 1),
            normed2, d_out, near_up, far_mlp[1], far_mlp2[1], down_w, upb[:, 2 * fp:], h)
        m1 = start(y_swap(send), keep, [fp, half], [False, True])
        have = {"h": h}

        def swap_h():
            have["h"] = line.do(core_swap, have["h"])

        def back_mid():
            have["d_middle"], d_branch, have["sums2"] = line.do(
                lambda p, m, d, g: rows_call(
                    kernel(back_middle_kernel), scalars, [cube(p), m, d], [g],
                    [shaped(F32), shaped(BF, 2)], True, "back_middle"),
                have["h"], middle, out_grad, g2)
            have["d_branch"] = flat(d_branch)

        def swap_d():
            have["d_branch"] = line.do(core_swap, have["d_branch"])

        def to_heads():
            have["d_att"] = line.do(
                lambda d, w: dot(d, w, NT).astype(BF), have["d_branch"], out_full)

        def attention_back(first):
            have["d_raw", first], have["col", first] = line.do(
                lambda a, b, c: attend_back(a, b, c, seq, 2 * images, padded, first, pairs),
                raw, have["d_att"], logs[first // pairs])

        def d_raws():
            return have["d_raw", 0], have["d_raw", pairs]

        def q_send():
            have["q_got"] = y_swap(line.do(
                lambda n, a, b: pair_sums(n, a, b, 1), normed1, *d_raws()))

        def q_keep():
            keep = line.do(lambda n, a, b: pair_sums(n, a, b, 0), normed1, *d_raws())
            have["q"] = start(have["q_got"], keep, [half, half], [True, True])

        def to_input():
            have["h"] = line.do(back_in, *d_raws(), qkv_full)

        def leave():
            token_grad, have["sums1"] = line.do(
                lambda p, a, m, g, token: rows_call(
                    kernel(leave_kernel), jnp.concatenate([y[None], token]).astype(jnp.int32),
                    [cube(p), a, m], [g], [jax.ShapeDtypeStruct(tokens.shape, BF)], True, "leave"),
                have["h"], tokens, have["d_middle"], g1, line.token)
            line.token = token_grad

        def small_sums():
            v = line.do(
                lambda *v: vectors_call(
                    core, *v[:4], v[4:], offsets, quarter, small.shape[1] - 128, pairs),
                have["sums1"], have["sums2"], have["col", 0], have["col", pairs], up_sum, up_sum2)
            sent, have["v"] = line.do(lambda v: (for_core(v, 1 - c), for_core(v, c)), v)
            have["v_got"] = core_permute(sent)

        def small_y():
            sent, have["v"] = line.do(lambda a, b: of_y(a + b), have["v"], have["v_got"])
            have["v_got"] = y_swap(sent)

        def out_send():
            sent, have["o"] = line.do(
                lambda a, b, d: out_sums(place_at[1:], a, b, d), *attended, have["d_branch"])
            have["o_got"] = y_swap(sent)

        def below(top, v):
            v = v.reshape(-1, width).astype(BF)
            return jnp.concatenate([top, jnp.pad(v, ((0, 32 - v.shape[0]), (0, 0)))], 0)

        def rest():
            have["r"] = start(
                line.do(below, have["o_got"], have["v_got"]), line.do(below, have["o"], have["v"]),
                [quarter, 32], [False, False])

        def rest_back():
            r = have["r"]
            r.add()
            for swap in swaps["rest"]:
                r.got = swap(r.keep)
                r.add()
            r.got = swaps["x"](r.keep)

        def to_mixed():
            have["mlp"] = line.do(
                lambda *v: feed_out(place_at, *v, 1),
                act, act2, down, down_w, far_mlp[1], far_mlp2[1])

        def swap_mixed():
            have["mlp_got"] = core_permute(line.do(lambda v: for_core(v, 1 - c), have["mlp"]))

        def mixed():
            have["mixed"] = line.do(
                lambda v, got, m, d: (
                    m + (up32(for_core(v, c)) + up32(got)).reshape(m.shape) + d).astype(BF)[:, :seq],
                have["mlp"], have["mlp_got"], middle, db)

        def grad_down():
            have["down"] = line.do(
                lambda *v: halves(x[None].astype(jnp.int32), v, fp // 2),
                m0.keep, m0.got, m1.keep, m1.got)

        def grad_up():
            where = [(2 * side + core) * ffq + k * fp
                     for k in range(parts) for core in (c, 1 - c) for side in (0, 1)]
            moves = []
            for k in range(parts):
                for side in (0, 1):
                    moves.append(((3 * k, 3 * k + 1), m0.sizes[0], side * fp, fp, 4 * k + side))
                    moves.append(((3 * k + 2,), 0, side * fp, fp, 4 * k + 2 + side))
            have["up"] = line.do(
                lambda *v: place(x, where, v, quarter, ff, moves),
                m0.keep, m0.got, m0.other, m1.keep, m1.got, m1.other)

        plain = {
            "swap_h": swap_h, "swap_in": swap_h, "back_mid": back_mid, "swap_d": swap_d, "to_heads": to_heads,
            "attend_0": lambda: attention_back(0), "attend_1": lambda: attention_back(pairs),
            "q_send": q_send, "q_keep": q_keep, "to_input": to_input, "leave": leave,
            "small_sums": small_sums, "small_y": small_y, "out_send": out_send, "rest": rest,
            "rest_back": rest_back, "to_mixed": to_mixed, "swap_mixed": swap_mixed, "mixed": mixed,
            "grad_down": grad_down, "grad_up": grad_up,
        }
        have.update(m0=m0, m1=m1)
        for name in ORDER:
            if name in plain:
                plain[name]()
                continue
            piece, step = name.split(".")
            piece = have[piece]
            if step in ("back", "join", "over"):
                {"back": piece.back, "join": piece.join, "over": piece.cross_over}[step]()
            elif step == "z2":
                piece.exchange("z2")
            elif step == "zz":
                piece.exchange("z1")
            else:
                piece.halve(step)
        q, rest, mixed, gd, gu = [have[name] for name in ("q", "r", "mixed", "down", "up")]

        where = qkv_starts(c) + qkv_starts(1 - c)
        moves = []
        for core in (0, 1):
            for side in (0, 1):
                for g in range(3 * pairs):
                    moves.append((((0, 1), (2,))[core], side * quarter, g * PAIR, PAIR,
                                  6 * pairs * core + 3 * pairs * side + g))
        gq = line.do(
            lambda *v: place(x, where, v, quarter, 3 * width, moves), q.keep, q.got, q.other)
        def in_halves(keep, got):
            n = quarter // 2
            out = [pick(keep[:n], got[:n], x), pick(got[:n], keep[:n], x)]
            v = [pick(keep[n:], got[n:], x), pick(got[n:], keep[n:], x)]
            return up32(jnp.concatenate(out, 0)), up32(jnp.concatenate(v, 0)).reshape(-1)

        go, vectors = line.do(in_halves, rest.keep, rest.got)
        token_grad = line.token

        cuts = [vectors[offsets[i]:offsets[i] + quarter] for i in range(6)]
        v_g1, v_b1, v_ob, v_g2, v_b2, v_db = cuts
        v_qv = vectors[offsets[6]:offsets[7]]
        v_ub = vectors[offsets[7]:offsets[7] + ffq]
        return (
            mixed, token_grad, v_g1, v_b1, gq, v_qv, go, v_ob, v_g2, v_b2, gu, v_ub, gd, v_db,
        )

    return per_device


def solution(mesh):
    rows = P(("rep", "shard"), None, None)
    vec, mat = P("shard"), P("shard", None)
    return jax.shard_map(
        build(mesh),
        mesh=mesh,
        in_specs=(rows, rows, P(("rep", "shard")), vec, vec, mat, vec, mat, vec, vec, vec,
                  mat, vec, mat, vec),
        out_specs=(rows, rows, vec, vec, mat, vec, mat, vec, vec, vec, mat, vec, mat, vec),
        check_vma=False,
    )
```
